128 devices in a mesh: rows: 16 (over z, x_lo, core), pairs: 8 (over x_hi, y).
Axes of the slice: x: 4 (x_hi: 2, x_lo: 2; x = x_hi * 2 + x_lo), y: 4, z: 4, core: 2. Of those that a mesh axis runs over, the one named last changes fastest.
Arguments:
- observed: float32 [24576, 4096], P('rows', 'pairs'), as said below
- estimate: float32 [24576, 4096], P('rows', 'pairs'), may hold values from -0.03827328 to 0.03827328
- mask: int32 [24576, 4096], P('rows', 'pairs'), may hold values from 0 to 1
- threshold: float32 [4096], P('pairs'), may hold values from 0.02 to 0.12
Outputs:
- regrouped: float32 [4096, 24576], P(('rows', 'pairs'))
The draws below stay inside these ranges and needn't reach their ends.
Inputs may be any that keep to these rules, and one draw needn't show every extreme that they name: observed has entries of order 24576^-1/2.
All inputs are finite; a program needn't handle non-finite values.
Results may differ from the reference program's by a relative error of at most 0.0003.
Values sent between devices are 32-bit elements; how exact they have to be, the bound alone decides.
No kernel may reach another device: no remote copies, remote signals or barrier semaphores. Data moves between devices by JAX's collectives and lax.ppermute only.
A program may use at most 128 MiB of HBM per device.

```python
import jax
import jax.numpy as jnp
from jax import lax

BW = 128
ROUNDS = 4
NS_STEPS = 3
ROWS = 24576
COLS = 4096
N_PAIRS = 8


def draw_observed(key, part):
    key_noise = jax.random.fold_in(key, 11)
    key_shared = jax.random.fold_in(key, 12)
    key_scale = jax.random.fold_in(key, 13)
    groups = COLS // (2 * BW)
    noise = jax.random.normal(key_noise, (ROWS, COLS), jnp.float32)
    shared = jax.random.normal(key_shared, (ROWS, groups, 1, BW), jnp.float32)
    colscale = jax.random.uniform(key_scale, (COLS,), jnp.float32, 0.6, 1.6)
    shared = jnp.broadcast_to(shared, (ROWS, groups, 2, BW)).reshape(ROWS, COLS)
    values = (noise + 0.7 * shared) * colscale[None, :] / jnp.sqrt(1.49 * ROWS)
    return values.astype(jnp.float32)


def touch_ends(array, rng, low, high):
    shape = array.shape
    place = [jax.random.randint(jax.random.fold_in(rng, axis), (), 0, shape[axis]) for axis in range(len(shape))]
    array = array.at[tuple(place)].set(low)
    longest = shape.index(max(shape))
    place[longest] = (place[longest] + 1) % shape[longest]
    return array.at[tuple(place)].set(high)


def block_levels(key, shape, shards, least, top_value):
    level = 1.0
    for dim, blocks in shards:
        steps = jax.random.uniform(jax.random.fold_in(jax.random.fold_in(key, 6), dim), (blocks,), jnp.float32, least / len(shards), top_value / len(shards))
        level = level * jnp.repeat(jnp.exp(steps), shape[dim] // blocks).reshape((-1,) + (1,) * (len(shape) - 1 - dim))
    return level


def centred(stream_key, extent, scale, limit, split=(), kind=jnp.bfloat16):
    drawn = scale * jax.random.normal(stream_key, extent, jnp.float32)
    if split:
        drawn = drawn * block_levels(stream_key, extent, split, -0.22, 0.18)
    return jnp.clip(drawn, -limit, limit).astype(kind)


def setup_inputs(seed: int = 0) -> dict:
    key_list = jax.random.split(jax.random.key(seed), 5)
    observed = draw_observed(jax.random.fold_in(key_list[4], 71), 0)
    estimate = centred(key_list[1], (ROWS, COLS), (ROWS ** -0.5), 0.03827328, ((0, 16), (1, 8)), jnp.float32)
    mask = touch_ends(jax.random.randint(key_list[2], (ROWS, COLS), 0, 2), jax.random.fold_in(key_list[2], 1), 0, 1).astype(jnp.int32)
    threshold = jnp.clip(0.02 + 0.09999999776482582 * jax.random.uniform(key_list[3], (COLS,), jnp.float32) ** block_levels(key_list[3], (COLS,), ((0, 8),), -0.2, 0.2), 0.02, 0.12)
    return {"observed": observed, "estimate": estimate, "mask": mask, "threshold": threshold}


HI = lax.Precision.HIGHEST

def whitening_of(gram):
    width = gram.shape[-1]
    eye = jnp.eye(width, dtype=jnp.float32)
    dsum = jnp.diagonal(gram, axis1=-2, axis2=-1) + 1e-06
    inv_root = 1.0 / jnp.sqrt(dsum)
    normed = gram * inv_root[..., :, None] * inv_root[..., None, :]
    fro = jnp.sqrt(lax.optimization_barrier(jnp.sum(normed * normed, axis=(-2, -1))))
    ymat = normed / fro[..., None, None]
    zmat = jnp.broadcast_to(eye, normed.shape)
    for step in range(NS_STEPS):
        tmat = 1.5 * eye - 0.5 * jnp.einsum('...ij,...jk->...ik', zmat, ymat, precision=HI)
        ymat = jnp.einsum('...ij,...jk->...ik', ymat, tmat, precision=HI)
        zmat = jnp.einsum('...ij,...jk->...ik', tmat, zmat, precision=HI)
    return inv_root[..., :, None] * zmat * jnp.sqrt(dsum)[..., None, :] / jnp.sqrt(fro)[..., None, None]

def reference(observed, estimate, mask, threshold):
    filled = jnp.where(mask == 1, observed, estimate)
    total = filled.shape[0]
    groups = N_PAIRS
    blocks = filled.reshape(total, groups, 4, BW)
    for round_index in range(ROUNDS):
        pairs = blocks.reshape(total, groups, 2, 2 * BW)
        gram = jnp.einsum('rdpi,rdpj->dpij', pairs, pairs, precision=HI)
        whitening = whitening_of(gram)
        pairs = jnp.einsum('rdpi,dpij->rdpj', pairs, whitening, precision=HI)
        blocks = pairs.reshape(total, groups, 4, BW)
        if round_index + 1 < ROUNDS:
            first = blocks[:, :, 1]
            third = blocks[:, :, 3]
            blocks = jnp.stack([blocks[:, :, 0], jnp.roll(third, 1, axis=1), blocks[:, :, 2], first], axis=2)
    filled = blocks.reshape(total, groups * 4 * BW)
    col_norm = jnp.sqrt(lax.optimization_barrier(jnp.sum(filled * filled, axis=0)) + 1e-06)
    factor = jnp.maximum(col_norm - threshold, 0.0) / col_norm
    shrunk = filled * factor[None, :]
    return shrunk.reshape(total, groups, 4 * BW).transpose(2, 1, 0).reshape(groups * 4 * BW, total)
```

```python
import functools

import jax
import jax.numpy as jnp
from jax import lax
from jax.experimental import pallas as pl
from jax.experimental.pallas import tpu as pltpu
from jax.sharding import Mesh, PartitionSpec as P

ROUNDS = 4
BW = 128
PW = 2 * BW
RH = 1536
RB = 2 * RH
CH = 512
AXES = ("zx", "core", "pairs")
F32 = jnp.float32
BF16 = jnp.bfloat16
VMEM = pl.BlockSpec(memory_space=pltpu.VMEM)
SMEM = pl.BlockSpec(memory_space=pltpu.SMEM)
NN = (((1,), (0,)), ((), ()))
NT = (((1,), (1,)), ((), ()))


def params():
    return pltpu.CompilerParams(vmem_limit_bytes=44 * 1024 * 1024)


def cost(flops, moved):
    return pl.CostEstimate(flops=flops, bytes_accessed=moved, transcendentals=0)


def split(x):
    high = x.astype(BF16)
    return high, (x - high.astype(F32)).astype(BF16)


def mxu(a, b, dims=NN):
    return lax.dot_general(a, b, dims, preferred_element_type=F32)


def dot3(a, b):
    (ah, al), (bh, bl) = a, b
    return mxu(ah, bh) + (mxu(ah, bl) + mxu(al, bh))


def fill_kernel(core_ref, obs_ref, est_ref, mask_ref, keep_ref, send_ref):
    filled = jnp.where(mask_ref[...] == 1, obs_ref[...], est_ref[...])
    first = core_ref[0] == 0
    a = filled[:, :PW]
    b = filled[:, PW:]
    keep_ref[...] = jnp.where(first, a, b).T
    send_ref[...] = jnp.where(first, b, a).T


def fill(core, observed, estimate, mask):
    step = 256
    rows = pl.BlockSpec((step, 2 * PW), lambda i: (i, 0))
    out = pl.BlockSpec((PW, step), lambda i: (0, i))
    return pl.pallas_call(
        fill_kernel,
        grid=(RH // step,),
        in_specs=[SMEM, rows, rows, rows],
        out_specs=[out, out],
        out_shape=[jax.ShapeDtypeStruct((PW, RH), F32)] * 2,
        compiler_params=params(),
        cost_estimate=cost(10**6, 15 * 10**6),
        name="fill",
    )(core, observed, estimate, mask)


def gram_parts(x_ref):
    hh = jnp.zeros((PW, PW), F32)
    hl = jnp.zeros((PW, PW), F32)
    for j in range(0, RH, CH):
        h, l = split(x_ref[:, j : j + CH])
        hh += mxu(h, h, NT)
        hl += mxu(h, l, NT)
    return hh, hl


def gram_first_kernel(x_ref, hh_ref, hl_ref):
    hh_ref[...], hl_ref[...] = gram_parts(x_ref)


def gram_second_kernel(x_ref, hh_ref, hl_ref, out_ref):
    hh, hl = gram_parts(x_ref)
    hl += hl_ref[...]
    g = hh + hh_ref[...] + (hl + hl.T)
    out_ref[0:BW] = g[:BW, :BW]
    out_ref[BW : 2 * BW] = g[:BW, BW:]
    out_ref[2 * BW : 3 * BW] = g[BW:, BW:]


def gram_cross_kernel(k_ref, m_ref, out_ref):
    total = jnp.zeros((PW, PW), F32)
    for half in range(2):
        for j in range(0, RH, CH):
            ka = half * RH + j
            ma = (1 - half) * RH + j
            k = jnp.concatenate(split(k_ref[:, ka : ka + CH]), axis=0)
            m = jnp.concatenate(split(m_ref[:, ma : ma + CH]), axis=0)
            total += mxu(k, m, NT)
    out_ref[...] = (total[:BW, :BW] + total[BW:, BW:]) + (total[:BW, BW:] + total[BW:, :BW])


def gram_first(x):
    return pl.pallas_call(
        gram_first_kernel,
        in_specs=[VMEM],
        out_specs=[VMEM] * 2,
        out_shape=[jax.ShapeDtypeStruct((PW, PW), F32)] * 2,
        compiler_params=params(),
        cost_estimate=cost(4 * RH * PW * PW, 3 * 10**6),
        name="gram_first",
    )(x)


def gram_second(x, hh, hl):
    return pl.pallas_call(
        gram_second_kernel,
        in_specs=[VMEM] * 3,
        out_specs=VMEM,
        out_shape=jax.ShapeDtypeStruct((3 * BW, BW), F32),
        compiler_params=params(),
        cost_estimate=cost(4 * RH * PW * PW, 3 * 10**6),
        name="gram_second",
    )(x, hh, hl)


def gram_cross(k, m):
    return pl.pallas_call(
        gram_cross_kernel,
        in_specs=[VMEM] * 2,
        out_specs=VMEM,
        out_shape=jax.ShapeDtypeStruct((BW, BW), F32),
        compiler_params=params(),
        cost_estimate=cost(4 * RH * PW * PW, 3 * 10**6),
        name="gram_cross",
    )(k, m)


def newton(gram):
    at_row = lax.broadcasted_iota(jnp.int32, (PW, PW), 0)
    at_col = lax.broadcasted_iota(jnp.int32, (PW, PW), 1)
    on = at_row == at_col
    diag = jnp.where(on, gram, 0.0)
    d_col = jnp.sum(diag, axis=1, keepdims=True) + 1e-06
    d_row = jnp.sum(diag, axis=0, keepdims=True) + 1e-06
    inv_col = 1.0 / jnp.sqrt(d_col)
    inv_row = 1.0 / jnp.sqrt(d_row)
    normed = gram * inv_col * inv_row
    fro = jnp.sqrt(jnp.sum(jnp.sum(normed * normed, axis=1, keepdims=True), axis=0, keepdims=True))
    y = normed / fro
    three = jnp.where(on, 1.5, 0.0)
    t = three - 0.5 * y
    ts = split(t)
    y = dot3(split(y), ts)
    z, zs = t, ts
    ys = split(y)
    t = three - 0.5 * dot3(zs, ys)
    ts = split(t)
    y = dot3(ys, ts)
    z = dot3(ts, zs)
    ys, zs = split(y), split(z)
    t = three - 0.5 * dot3(zs, ys)
    ts = split(t)
    z = dot3(ts, zs)
    return z, y, t, d_col, d_row, inv_row, fro


def gram_of(g_refs, diag_refs):
    total = (g_refs[0][...] + g_refs[1][...]) + (g_refs[2][...] + g_refs[3][...])
    if diag_refs:
        d0, cross, d1 = diag_refs[0][...], total, diag_refs[1][...]
    else:
        d0, cross, d1 = total[:BW], total[BW : 2 * BW], total[2 * BW :]
    top = jnp.concatenate([d0, cross], axis=1)
    bottom = jnp.concatenate([cross.T, d1], axis=1)
    return jnp.concatenate([top, bottom], axis=0)


def columns(x_refs, first, half, j):
    if first:
        return x_refs[half][:, j : j + CH]
    ka = half * RH + j
    ma = (1 - half) * RH + j
    return jnp.concatenate([x_refs[0][:, ka : ka + CH], x_refs[1][:, ma : ma + CH]], axis=0)


def apply_to(w, x_refs, first, out_ref, offset=None):
    wh, wl = split(w)
    both = jnp.concatenate([wh, wl], axis=0)
    for half in range(2):
        for j in range(0, RH, CH):
            xh, xl = split(columns(x_refs, first, half, j))
            wide = mxu(both, xh)
            value = wide[:BW] + (wide[BW:] + mxu(wh, xl))
            if offset is None:
                out_ref[:, half * RH + j : half * RH + j + CH] = value
            else:
                at = pl.multiple_of((offset if half == 0 else RH - offset) + j, 128)
                out_ref[:, pl.ds(at, CH)] = value


def whiten_kernel(first, *refs):
    n = 4 if first else 6
    g_refs, diag_refs = refs[:4], refs[4:n]
    x_refs = refs[n : n + 2]
    moved_ref, w_ref, z_ref, y_ref, t_ref, d_ref = refs[n + 2 :]
    z, y, t, d_col, d_row, inv_row, fro = newton(gram_of(g_refs, diag_refs))
    wt = jnp.sqrt(d_col) * z.T * (inv_row / jnp.sqrt(fro))
    apply_to(wt[BW:], x_refs, first, moved_ref)
    w_ref[...] = wt[:BW]
    z_ref[...] = z
    y_ref[...] = y
    t_ref[...] = t
    root = jnp.sqrt(d_col) * jnp.sqrt(d_row)
    d_ref[...] = jnp.concatenate([root[:BW, :BW], root[BW:, BW:]], axis=0)


def whiten(grams, diags, xs, first):
    args = [*grams, *diags, *xs]
    return pl.pallas_call(
        functools.partial(whiten_kernel, first),
        in_specs=[VMEM] * len(args),
        out_specs=[VMEM] * 6,
        out_shape=[
            jax.ShapeDtypeStruct((BW, RB), F32),
            jax.ShapeDtypeStruct((BW, PW), F32),
            jax.ShapeDtypeStruct((PW, PW), F32),
            jax.ShapeDtypeStruct((PW, PW), F32),
            jax.ShapeDtypeStruct((PW, PW), F32),
            jax.ShapeDtypeStruct((PW, BW), F32),
        ],
        compiler_params=params(),
        cost_estimate=cost(10**9, 6 * 10**6),
        name="whiten",
    )(*args)


def kept_kernel(first, *refs):
    w_ref, z_ref, y_ref, t_ref, d_ref = refs[:5]
    x_refs = refs[5:7]
    kept_ref, kept_diag_ref, moved_diag_ref = refs[7:]
    zs = split(z_ref[...])
    ys = split(dot3(split(y_ref[...]), split(t_ref[...])))
    new = dot3(ys, zs)
    kept_diag_ref[...] = new[:BW, :BW] * d_ref[:BW]
    moved_diag_ref[...] = new[BW:, BW:] * d_ref[BW:]
    apply_to(w_ref[...], x_refs, first, kept_ref)


def kept_part(w, z, y, t, d, xs, first):
    return pl.pallas_call(
        functools.partial(kept_kernel, first),
        in_specs=[VMEM] * 7,
        out_specs=[VMEM] * 3,
        out_shape=[
            jax.ShapeDtypeStruct((BW, RB), F32),
            jax.ShapeDtypeStruct((BW, BW), F32),
            jax.ShapeDtypeStruct((BW, BW), F32),
        ],
        compiler_params=params(),
        cost_estimate=cost(10**9, 6 * 10**6),
        name="kept",
    )(w, z, y, t, d, *xs)


def by_core(w, even):
    parts = [w[i : i + 32] for i in range(0, PW, 32)]
    evens = jnp.concatenate(parts[0::2], axis=0)
    odds = jnp.concatenate(parts[1::2], axis=0)
    return jnp.where(even, evens, odds)


def last_kernel(core_ref, thr_ref, *refs):
    g_refs, diag_refs, x_refs = refs[:4], refs[4:6], refs[6:8]
    send_ref, w_ref = refs[8:]
    core = core_ref[0]
    z, y, t, d_col, d_row, inv_row, fro = newton(gram_of(g_refs, diag_refs))
    y = dot3(split(y), split(t))
    norm = jnp.sqrt(d_col * jnp.sum(z * y, axis=1, keepdims=True) + 1e-06)
    at_row = lax.broadcasted_iota(jnp.int32, (PW, PW), 0)
    at_col = lax.broadcasted_iota(jnp.int32, (PW, PW), 1)
    thr_row = jnp.where(core == 0, thr_ref[:, :PW], thr_ref[:, PW:])
    thr = jnp.sum(jnp.where(at_row == at_col, thr_row, 0.0), axis=1, keepdims=True)
    factor = jnp.maximum(norm - thr, 0.0) / norm
    wt = (factor * jnp.sqrt(d_col)) * z.T * (inv_row / jnp.sqrt(fro))
    apply_to(by_core(wt, core != 0), x_refs, False, send_ref, core * RH)
    w_ref[...] = by_core(wt, core == 0)


def last(core, thr, grams, diags, xs):
    return pl.pallas_call(
        last_kernel,
        in_specs=[SMEM] + [VMEM] * 9,
        out_specs=[VMEM] * 2,
        out_shape=[jax.ShapeDtypeStruct((BW, RB), F32), jax.ShapeDtypeStruct((BW, PW), F32)],
        compiler_params=params(),
        cost_estimate=cost(10**9, 6 * 10**6),
        name="last",
    )(core, thr, *grams, *diags, *xs)


def last_kept_kernel(core_ref, w_ref, k_ref, m_ref, out_ref):
    apply_to(w_ref[...], (k_ref, m_ref), False, out_ref, core_ref[0] * RH)


def last_kept(core, w, xs):
    return pl.pallas_call(
        last_kept_kernel,
        in_specs=[SMEM] + [VMEM] * 3,
        out_specs=VMEM,
        out_shape=jax.ShapeDtypeStruct((BW, RB), F32),
        compiler_params=params(),
        cost_estimate=cost(10**9, 6 * 10**6),
        name="last_kept",
    )(core, w, *xs)


def to(block, where):
    route = []
    for i in range(8):
        for c in range(2):
            for g in range(8):
                ti, tc, tg = where(i, c, g)
                route.append(((i * 2 + c) * 8 + g, (ti * 2 + tc) * 8 + tg))
    return lax.ppermute(block, AXES, route)


def swap_cores(block):
    return to(block, lambda i, c, g: (i, 1 - c, g))


def onward(block):
    return to(block, lambda i, c, g: (i, 1, g) if c == 0 else (i, 0, (g + 1) % 8))


def reduced(partial):
    pair = partial + to(partial, lambda i, c, g: (i ^ 1, c, g))
    return [pair] + [to(pair, lambda i, c, g, k=k: (i ^ k, c, g)) for k in (2, 4, 6)]


def on_device(observed, estimate, mask, threshold):
    core_index = lax.axis_index("core")
    core = core_index.reshape(1).astype(jnp.int32)
    thr = threshold.reshape(1, -1)
    keep, send = fill(core, observed, estimate, mask)
    got = swap_cores(send)
    grams = reduced(gram_second(got, *gram_first(keep)))
    xs, diags = (keep, got), []
    for round_index in range(ROUNDS - 1):
        first = round_index == 0
        moved, *rest = whiten(grams, diags, xs, first)
        arrived = onward(moved)
        kept, kept_diag, moved_diag = kept_part(*rest, xs, first)
        diags = [kept_diag, onward(moved_diag)]
        xs = (kept, arrived)
        grams = reduced(gram_cross(*xs))
    send, w = last(core, thr, grams, diags, xs)
    got = swap_cores(send)
    keep = last_kept(core, w, xs)
    low = jnp.where(core_index == 0, keep, got)
    high = jnp.where(core_index == 0, got, keep)
    packed = jnp.concatenate([low, high], axis=0).reshape(64, 4, RB)
    landed = lax.all_to_all(packed, ("zx", "pairs"), split_axis=0, concat_axis=0, tiled=True)
    landed = landed.reshape(8, 8, 4, RB).transpose(2, 1, 0, 3)
    return landed.reshape(32, 8 * RB)


def solution(mesh):
    finer = Mesh(mesh.devices.reshape(8, 2, 8), AXES)
    placed = P(("zx", "core"), "pairs")
    return jax.shard_map(
        on_device,
        mesh=finer,
        in_specs=(placed, placed, placed, P("pairs")),
        out_specs=P(AXES, None),
        check_vma=False,
    )
```

```python
import functools

import jax
import jax.numpy as jnp
from jax import lax
from jax.experimental import pallas as pl
from jax.experimental.pallas import tpu as pltpu
from jax.sharding import Mesh, PartitionSpec as P

ROUNDS = 4
BW = 128
PW = 2 * BW
RH = 1536
RB = 2 * RH
CH = 512
AXES = ("zx", "core", "pairs")
F32 = jnp.float32
BF16 = jnp.bfloat16
VMEM = pl.BlockSpec(memory_space=pltpu.VMEM)
SMEM = pl.BlockSpec(memory_space=pltpu.SMEM)
NN = (((1,), (0,)), ((), ()))
NT = (((1,), (1,)), ((), ()))


def params(mib=44):
    return pltpu.CompilerParams(vmem_limit_bytes=mib * 1024 * 1024)


def cost(flops, moved):
    return pl.CostEstimate(flops=flops, bytes_accessed=moved, transcendentals=0)


def split(x):
    high = x.astype(BF16)
    return high, (x - high.astype(F32)).astype(BF16)


def mxu(a, b, dims=NN):
    return lax.dot_general(a, b, dims, preferred_element_type=F32)


def dot3(a, b):
    (ah, al), (bh, bl) = a, b
    return mxu(ah, bh) + (mxu(ah, bl) + mxu(al, bh))


def fill_kernel(core_ref, obs_ref, est_ref, mask_ref, keep_ref, send_ref):
    filled = jnp.where(mask_ref[...] == 1, obs_ref[...], est_ref[...])
    first = core_ref[0] == 0
    a = filled[:, :PW]
    b = filled[:, PW:]
    keep_ref[...] = jnp.where(first, a, b).T
    send_ref[...] = jnp.where(first, b, a).T


def fill(core, observed, estimate, mask):
    step = 256
    rows = pl.BlockSpec((step, 2 * PW), lambda i: (i, 0))
    out = pl.BlockSpec((PW, step), lambda i: (0, i))
    return pl.pallas_call(
        fill_kernel,
        grid=(RH // step,),
        in_specs=[SMEM, rows, rows, rows],
        out_specs=[out, out],
        out_shape=[jax.ShapeDtypeStruct((PW, RH), F32)] * 2,
        compiler_params=params(60),
        cost_estimate=cost(10**6, 15 * 10**6),
        name="fill",
    )(core, observed, estimate, mask)


def gram_parts(x_ref):
    hh = jnp.zeros((PW, PW), F32)
    hl = jnp.zeros((PW, PW), F32)
    for j in range(0, RH, CH):
        h, l = split(x_ref[:, j : j + CH])
        hh += mxu(h, h, NT)
        hl += mxu(h, l, NT)
    return hh, hl


def gram_first_kernel(x_ref, hh_ref, hl_ref):
    hh_ref[...], hl_ref[...] = gram_parts(x_ref)


def gram_second_kernel(x_ref, hh_ref, hl_ref, out_ref):
    hh, hl = gram_parts(x_ref)
    hl += hl_ref[...]
    g = hh + hh_ref[...] + (hl + hl.T)
    at_row = lax.broadcasted_iota(jnp.int32, (BW, BW), 0)
    at_col = lax.broadcasted_iota(jnp.int32, (BW, BW), 1)
    d0, d1 = g[:BW, :BW], g[BW:, BW:]
    out_ref[0:BW] = g[:BW, BW:]
    out_ref[BW : 2 * BW] = jnp.where(at_col > at_row, d0, d1)
    on_diag = jnp.sum(jnp.where(at_col == at_row, d0, 0.0), axis=0, keepdims=True)
    out_ref[2 * BW :] = jnp.broadcast_to(on_diag, (8, BW))


def gram_cross_kernel(k_ref, m_ref, out_ref):
    total = jnp.zeros((PW, PW), F32)
    for half in range(2):
        for j in range(0, RH, CH):
            ka = half * RH + j
            ma = (1 - half) * RH + j
            k = jnp.concatenate(split(k_ref[:, ka : ka + CH]), axis=0)
            m = jnp.concatenate(split(m_ref[:, ma : ma + CH]), axis=0)
            total += mxu(k, m, NT)
    out_ref[...] = (total[:BW, :BW] + total[BW:, BW:]) + (total[:BW, BW:] + total[BW:, :BW])


def gram_first(x):
    return pl.pallas_call(
        gram_first_kernel,
        in_specs=[VMEM],
        out_specs=[VMEM] * 2,
        out_shape=[jax.ShapeDtypeStruct((PW, PW), F32)] * 2,
        compiler_params=params(),
        cost_estimate=cost(4 * RH * PW * PW, 3 * 10**6),
        name="gram_first",
    )(x)


def gram_second(x, hh, hl):
    return pl.pallas_call(
        gram_second_kernel,
        in_specs=[VMEM] * 3,
        out_specs=VMEM,
        out_shape=jax.ShapeDtypeStruct((2 * BW + 8, BW), F32),
        compiler_params=params(),
        cost_estimate=cost(4 * RH * PW * PW, 3 * 10**6),
        name="gram_second",
    )(x, hh, hl)


def gram_cross(k, m):
    return pl.pallas_call(
        gram_cross_kernel,
        in_specs=[VMEM] * 2,
        out_specs=VMEM,
        out_shape=jax.ShapeDtypeStruct((BW, BW), F32),
        compiler_params=params(),
        cost_estimate=cost(4 * RH * PW * PW, 3 * 10**6),
        name="gram_cross",
    )(k, m)


def newton(gram):
    at_row = lax.broadcasted_iota(jnp.int32, (PW, PW), 0)
    at_col = lax.broadcasted_iota(jnp.int32, (PW, PW), 1)
    on = at_row == at_col
    diag = jnp.where(on, gram, 0.0)
    d_col = jnp.sum(diag, axis=1, keepdims=True) + 1e-06
    d_row = jnp.sum(diag, axis=0, keepdims=True) + 1e-06
    inv_col = 1.0 / jnp.sqrt(d_col)
    inv_row = 1.0 / jnp.sqrt(d_row)
    normed = gram * inv_col * inv_row
    fro = jnp.sqrt(jnp.sum(jnp.sum(normed * normed, axis=1, keepdims=True), axis=0, keepdims=True))
    y = normed / fro
    three = jnp.where(on, 1.5, 0.0)
    t = three - 0.5 * y
    ts = split(t)
    y = dot3(split(y), ts)
    z, zs = t, ts
    ys = split(y)
    t = three - 0.5 * dot3(zs, ys)
    ts = split(t)
    y = dot3(ys, ts)
    z = dot3(ts, zs)
    ys, zs = split(y), split(z)
    t = three - 0.5 * dot3(zs, ys)
    ts = split(t)
    z = dot3(ts, zs)
    return z, y, t, d_col, d_row, inv_row, fro


def gram_of(g_refs, diag_refs):
    total = (g_refs[0][...] + g_refs[1][...]) + (g_refs[2][...] + g_refs[3][...])
    if diag_refs:
        d0, cross, d1 = diag_refs[0][...], total, diag_refs[1][...]
    else:
        cross, both, on_diag = total[:BW], total[BW : 2 * BW], total[2 * BW : 2 * BW + 1]
        at_row = lax.broadcasted_iota(jnp.int32, (BW, BW), 0)
        at_col = lax.broadcasted_iota(jnp.int32, (BW, BW), 1)
        turned = both.T
        d0 = jnp.where(at_col == at_row, on_diag, jnp.where(at_col > at_row, both, turned))
        d1 = jnp.where(at_col > at_row, turned, both)
    top = jnp.concatenate([d0, cross], axis=1)
    bottom = jnp.concatenate([cross.T, d1], axis=1)
    return jnp.concatenate([top, bottom], axis=0)


def columns(x_refs, first, half, j):
    if first:
        return x_refs[half][:, j : j + CH]
    ka = half * RH + j
    ma = (1 - half) * RH + j
    return jnp.concatenate([x_refs[0][:, ka : ka + CH], x_refs[1][:, ma : ma + CH]], axis=0)


def apply_to(w, x_refs, first, out_ref, offset=None):
    wh, wl = split(w)
    both = jnp.concatenate([wh, wl], axis=0)
    for half in range(2):
        for j in range(0, RH, CH):
            xh, xl = split(columns(x_refs, first, half, j))
            wide = mxu(both, xh)
            value = wide[:BW] + (wide[BW:] + mxu(wh, xl))
            if offset is None:
                out_ref[:, half * RH + j : half * RH + j + CH] = value
            else:
                at = pl.multiple_of((offset if half == 0 else RH - offset) + j, 128)
                out_ref[:, pl.ds(at, CH)] = value


def whiten_kernel(first, *refs):
    n = 4 if first else 6
    g_refs, diag_refs = refs[:4], refs[4:n]
    x_refs = refs[n : n + 2]
    moved_ref, w_ref, z_ref, y_ref, t_ref, d_ref = refs[n + 2 :]
    z, y, t, d_col, d_row, inv_row, fro = newton(gram_of(g_refs, diag_refs))
    wt = jnp.sqrt(d_col) * z.T * (inv_row / jnp.sqrt(fro))
    apply_to(wt[BW:], x_refs, first, moved_ref)
    w_ref[...] = wt[:BW]
    z_ref[...] = z
    y_ref[...] = y
    t_ref[...] = t
    root = jnp.sqrt(d_col) * jnp.sqrt(d_row)
    d_ref[...] = jnp.concatenate([root[:BW, :BW], root[BW:, BW:]], axis=0)


def whiten(grams, diags, xs, first):
    args = [*grams, *diags, *xs]
    return pl.pallas_call(
        functools.partial(whiten_kernel, first),
        in_specs=[VMEM] * len(args),
        out_specs=[VMEM] * 6,
        out_shape=[
            jax.ShapeDtypeStruct((BW, RB), F32),
            jax.ShapeDtypeStruct((BW, PW), F32),
            jax.ShapeDtypeStruct((PW, PW), F32),
            jax.ShapeDtypeStruct((PW, PW), F32),
            jax.ShapeDtypeStruct((PW, PW), F32),
            jax.ShapeDtypeStruct((PW, BW), F32),
        ],
        compiler_params=params(),
        cost_estimate=cost(10**9, 6 * 10**6),
        name="whiten",
    )(*args)


def kept_kernel(first, *refs):
    w_ref, z_ref, y_ref, t_ref, d_ref = refs[:5]
    x_refs = refs[5:7]
    kept_ref, kept_diag_ref, moved_diag_ref = refs[7:]
    zs = split(z_ref[...])
    ys = split(dot3(split(y_ref[...]), split(t_ref[...])))
    new = dot3(ys, zs)
    kept_diag_ref[...] = new[:BW, :BW] * d_ref[:BW]
    moved_diag_ref[...] = new[BW:, BW:] * d_ref[BW:]
    apply_to(w_ref[...], x_refs, first, kept_ref)


def kept_part(w, z, y, t, d, xs, first):
    return pl.pallas_call(
        functools.partial(kept_kernel, first),
        in_specs=[VMEM] * 7,
        out_specs=[VMEM] * 3,
        out_shape=[
            jax.ShapeDtypeStruct((BW, RB), F32),
            jax.ShapeDtypeStruct((BW, BW), F32),
            jax.ShapeDtypeStruct((BW, BW), F32),
        ],
        compiler_params=params(),
        cost_estimate=cost(10**9, 6 * 10**6),
        name="kept",
    )(w, z, y, t, d, *xs)


def by_core(w, even):
    parts = [w[i : i + 32] for i in range(0, PW, 32)]
    evens = jnp.concatenate(parts[0::2], axis=0)
    odds = jnp.concatenate(parts[1::2], axis=0)
    return jnp.where(even, evens, odds)


def last_kernel(core_ref, thr_ref, *refs):
    g_refs, diag_refs, x_refs = refs[:4], refs[4:6], refs[6:8]
    send_ref, w_ref = refs[8:]
    core = core_ref[0]
    z, y, t, d_col, d_row, inv_row, fro = newton(gram_of(g_refs, diag_refs))
    y = dot3(split(y), split(t))
    norm = jnp.sqrt(d_col * jnp.sum(z * y, axis=1, keepdims=True) + 1e-06)
    at_row = lax.broadcasted_iota(jnp.int32, (PW, PW), 0)
    at_col = lax.broadcasted_iota(jnp.int32, (PW, PW), 1)
    thr_row = jnp.where(core == 0, thr_ref[:, :PW], thr_ref[:, PW:])
    thr = jnp.sum(jnp.where(at_row == at_col, thr_row, 0.0), axis=1, keepdims=True)
    factor = jnp.maximum(norm - thr, 0.0) / norm
    wt = (factor * jnp.sqrt(d_col)) * z.T * (inv_row / jnp.sqrt(fro))
    apply_to(by_core(wt, core != 0), x_refs, False, send_ref, core * RH)
    w_ref[...] = by_core(wt, core == 0)


def last(core, thr, grams, diags, xs):
    return pl.pallas_call(
        last_kernel,
        in_specs=[SMEM] + [VMEM] * 9,
        out_specs=[VMEM] * 2,
        out_shape=[jax.ShapeDtypeStruct((BW, RB), F32), jax.ShapeDtypeStruct((BW, PW), F32)],
        compiler_params=params(),
        cost_estimate=cost(10**9, 6 * 10**6),
        name="last",
    )(core, thr, *grams, *diags, *xs)


def last_kept_kernel(core_ref, w_ref, k_ref, m_ref, got_ref, out_ref):
    core = core_ref[0]
    mine = pl.multiple_of(core * BW, BW)
    apply_to(w_ref[...], (k_ref, m_ref), False, out_ref.at[pl.ds(mine, BW)], core * RH)
    out_ref[pl.ds(pl.multiple_of(BW - mine, BW), BW)] = got_ref[...]


def last_kept(core, w, xs, got):
    return pl.pallas_call(
        last_kept_kernel,
        in_specs=[SMEM] + [VMEM] * 4,
        out_specs=VMEM,
        out_shape=jax.ShapeDtypeStruct((PW, RB), F32),
        compiler_params=params(),
        cost_estimate=cost(10**9, 6 * 10**6),
        name="last_kept",
    )(core, w, *xs, got)


def to(block, where):
    route = []
    for i in range(8):
        for c in range(2):
            for g in range(8):
                ti, tc, tg = where(i, c, g)
                route.append(((i * 2 + c) * 8 + g, (ti * 2 + tc) * 8 + tg))
    return lax.ppermute(block, AXES, route)


def swap_cores(block):
    return to(block, lambda i, c, g: (i, 1 - c, g))


def onward(block):
    return to(block, lambda i, c, g: (i, 1, g) if c == 0 else (i, 0, (g + 1) % 8))


def reduced(partial):
    pair = partial + to(partial, lambda i, c, g: (i ^ 1, c, g))
    return [pair] + [to(pair, lambda i, c, g, k=k: (i ^ k, c, g)) for k in (2, 4, 6)]


def on_device(observed, estimate, mask, threshold):
    core_index = lax.axis_index("core")
    core = core_index.reshape(1).astype(jnp.int32)
    thr = threshold.reshape(1, -1)
    keep, send = fill(core, observed, estimate, mask)
    got = swap_cores(send)
    grams = reduced(gram_second(got, *gram_first(keep)))
    xs, diags = (keep, got), []
    for round_index in range(ROUNDS - 1):
        first = round_index == 0
        moved, *rest = whiten(grams, diags, xs, first)
        arrived = onward(moved)
        kept, kept_diag, moved_diag = kept_part(*rest, xs, first)
        diags = [kept_diag, onward(moved_diag)]
        xs = (kept, arrived)
        grams = reduced(gram_cross(*xs))
    send, w = last(core, thr, grams, diags, xs)
    got = swap_cores(send)
    packed = last_kept(core, w, xs, got).reshape(64, 4, RB)
    landed = lax.all_to_all(packed, ("zx", "pairs"), split_axis=0, concat_axis=0, tiled=True)
    landed = landed.reshape(8, 8, 4, RB).transpose(2, 1, 0, 3)
    return landed.reshape(32, 8 * RB)


def solution(mesh):
    finer = Mesh(mesh.devices.reshape(8, 2, 8), AXES)
    placed = P(("zx", "core"), "pairs")
    return jax.shard_map(
        on_device,
        mesh=finer,
        in_specs=(placed, placed, placed, P("pairs")),
        out_specs=P(AXES, None),
        check_vma=False,
    )
```

```python
import functools

import jax
import jax.numpy as jnp
from jax import lax
from jax.experimental import pallas as pl
from jax.experimental.pallas import tpu as pltpu
from jax.sharding import Mesh, PartitionSpec as P

ROUNDS = 4
BW = 128
PW = 2 * BW
RH = 1536
RB = 2 * RH
CH = 512
AXES = ("zx", "core", "pairs")
F32 = jnp.float32
BF16 = jnp.bfloat16
VMEM = pl.BlockSpec(memory_space=pltpu.VMEM)
ANY = pl.BlockSpec(memory_space=pl.ANY)
SMEM = pl.BlockSpec(memory_space=pltpu.SMEM)
NN = (((1,), (0,)), ((), ()))
NT = (((1,), (1,)), ((), ()))


def params(mib=44):
    return pltpu.CompilerParams(vmem_limit_bytes=mib * 1024 * 1024)


def cost(flops, moved):
    return pl.CostEstimate(flops=flops, bytes_accessed=moved, transcendentals=0)


def split(x):
    high = x.astype(BF16)
    return high, (x - high.astype(F32)).astype(BF16)


def mxu(a, b, dims=NN):
    return lax.dot_general(a, b, dims, preferred_element_type=F32)


def dot3(a, b):
    (ah, al), (bh, bl) = a, b
    return mxu(ah, bh) + (mxu(ah, bl) + mxu(al, bh))


def fill_kernel(core_ref, obs_ref, est_ref, mask_ref, keep_ref, send_ref):
    filled = jnp.where(mask_ref[...] == 1, obs_ref[...], est_ref[...])
    first = core_ref[0] == 0
    a = filled[:, :PW]
    b = filled[:, PW:]
    keep_ref[...] = jnp.where(first, a, b).T
    send_ref[...] = jnp.where(first, b, a).T


def fill(core, observed, estimate, mask):
    step = 256
    rows = pl.BlockSpec((step, 2 * PW), lambda i: (i, 0))
    out = pl.BlockSpec((PW, step), lambda i: (0, i))
    return pl.pallas_call(
        fill_kernel,
        grid=(RH // step,),
        in_specs=[SMEM, rows, rows, rows],
        out_specs=[out, out],
        out_shape=[jax.ShapeDtypeStruct((PW, RH), F32)] * 2,
        compiler_params=params(60),
        cost_estimate=cost(10**6, 15 * 10**6),
        name="fill",
    )(core, observed, estimate, mask)


def gram_parts(x_ref):
    hh = jnp.zeros((PW, PW), F32)
    hl = jnp.zeros((PW, PW), F32)
    for j in range(0, RH, CH):
        h, l = split(x_ref[:, j : j + CH])
        hh += mxu(h, h, NT)
        hl += mxu(h, l, NT)
    return hh, hl


def gram_first_kernel(x_ref, hh_ref, hl_ref):
    hh_ref[...], hl_ref[...] = gram_parts(x_ref)


def gram_second_kernel(x_ref, hh_ref, hl_ref, out_ref):
    hh, hl = gram_parts(x_ref)
    hl += hl_ref[...]
    g = hh + hh_ref[...] + (hl + hl.T)
    at_row = lax.broadcasted_iota(jnp.int32, (BW, BW), 0)
    at_col = lax.broadcasted_iota(jnp.int32, (BW, BW), 1)
    d0, d1 = g[:BW, :BW], g[BW:, BW:]
    out_ref[0:BW] = g[:BW, BW:]
    out_ref[BW : 2 * BW] = jnp.where(at_col > at_row, d0, d1)
    on_diag = jnp.sum(jnp.where(at_col == at_row, d0, 0.0), axis=0, keepdims=True)
    out_ref[2 * BW :] = jnp.broadcast_to(on_diag, (8, BW))


def gram_cross_kernel(k_ref, m_ref, *refs):
    out_ref = refs[-1]
    total = jnp.zeros((PW, PW), F32)
    for half in range(2):
        for j in range(0, RH, CH):
            ka = half * RH + j
            ma = (1 - half) * RH + j
            k = jnp.concatenate(split(k_ref[:, ka : ka + CH]), axis=0)
            m = jnp.concatenate(split(m_ref[:, ma : ma + CH]), axis=0)
            total += mxu(k, m, NT)
    out_ref[...] = (total[:BW, :BW] + total[BW:, BW:]) + (total[:BW, BW:] + total[BW:, :BW])


def gram_first(x):
    return pl.pallas_call(
        gram_first_kernel,
        in_specs=[VMEM],
        out_specs=[VMEM] * 2,
        out_shape=[jax.ShapeDtypeStruct((PW, PW), F32)] * 2,
        compiler_params=params(),
        cost_estimate=cost(4 * RH * PW * PW, 3 * 10**6),
        name="gram_first",
    )(x)


def gram_second(x, hh, hl):
    return pl.pallas_call(
        gram_second_kernel,
        in_specs=[VMEM] * 3,
        out_specs=VMEM,
        out_shape=jax.ShapeDtypeStruct((2 * BW + 8, BW), F32),
        compiler_params=params(),
        cost_estimate=cost(4 * RH * PW * PW, 3 * 10**6),
        name="gram_second",
    )(x, hh, hl)


def gram_cross(k, m, *arrived):
    return pl.pallas_call(
        gram_cross_kernel,
        in_specs=[VMEM] * 2 + [ANY] * len(arrived),
        out_specs=VMEM,
        out_shape=jax.ShapeDtypeStruct((BW, BW), F32),
        compiler_params=params(),
        cost_estimate=cost(4 * RH * PW * PW, 3 * 10**6),
        name="gram_cross",
    )(k, m, *arrived)


def newton(gram):
    at_row = lax.broadcasted_iota(jnp.int32, (PW, PW), 0)
    at_col = lax.broadcasted_iota(jnp.int32, (PW, PW), 1)
    on = at_row == at_col
    diag = jnp.where(on, gram, 0.0)
    d_col = jnp.sum(diag, axis=1, keepdims=True) + 1e-06
    d_row = jnp.sum(diag, axis=0, keepdims=True) + 1e-06
    inv_col = 1.0 / jnp.sqrt(d_col)
    inv_row = 1.0 / jnp.sqrt(d_row)
    normed = gram * inv_col * inv_row
    fro = jnp.sqrt(jnp.sum(jnp.sum(normed * normed, axis=1, keepdims=True), axis=0, keepdims=True))
    y = normed / fro
    three = jnp.where(on, 1.5, 0.0)
    t = three - 0.5 * y
    ts = split(t)
    y = dot3(split(y), ts)
    z, zs = t, ts
    ys = split(y)
    t = three - 0.5 * dot3(zs, ys)
    ts = split(t)
    y = dot3(ys, ts)
    z = dot3(ts, zs)
    ys, zs = split(y), split(z)
    t = three - 0.5 * dot3(zs, ys)
    ts = split(t)
    z = dot3(ts, zs)
    return z, y, t, d_col, d_row, inv_row, fro


def gram_of(g_refs, diag_refs):
    total = (g_refs[0][...] + g_refs[1][...]) + (g_refs[2][...] + g_refs[3][...])
    if diag_refs:
        d0, cross, d1 = diag_refs[0][...], total, diag_refs[1][...]
    else:
        cross, both, on_diag = total[:BW], total[BW : 2 * BW], total[2 * BW : 2 * BW + 1]
        at_row = lax.broadcasted_iota(jnp.int32, (BW, BW), 0)
        at_col = lax.broadcasted_iota(jnp.int32, (BW, BW), 1)
        turned = both.T
        d0 = jnp.where(at_col == at_row, on_diag, jnp.where(at_col > at_row, both, turned))
        d1 = jnp.where(at_col > at_row, turned, both)
    top = jnp.concatenate([d0, cross], axis=1)
    bottom = jnp.concatenate([cross.T, d1], axis=1)
    return jnp.concatenate([top, bottom], axis=0)


HALVES = "halves"
CROSSED = (False, True)
SHADOW = (True, False)
PLAIN = (False, False)


def columns(x_refs, form, half, j):
    if form == HALVES:
        return x_refs[half][:, j : j + CH]
    ats = [((1 - half) if crossed else half) * RH + j for crossed in form]
    return jnp.concatenate([x_ref[:, at : at + CH] for x_ref, at in zip(x_refs, ats)], axis=0)


def apply_to(w, x_refs, form, out_ref, offset=None):
    wh, wl = split(w)
    both = jnp.concatenate([wh, wl], axis=0)
    for half in range(2):
        for j in range(0, RH, CH):
            xh, xl = split(columns(x_refs, form, half, j))
            wide = mxu(both, xh)
            value = wide[:BW] + (wide[BW:] + mxu(wh, xl))
            if offset is None:
                out_ref[:, half * RH + j : half * RH + j + CH] = value
            else:
                at = pl.multiple_of((offset if half == 0 else RH - offset) + j, 128)
                out_ref[:, pl.ds(at, CH)] = value


BLOCK = jax.ShapeDtypeStruct((BW, RB), F32)
ROWS_OF_W = jax.ShapeDtypeStruct((BW, PW), F32)
SQUARE = jax.ShapeDtypeStruct((PW, PW), F32)
SCALES = jax.ShapeDtypeStruct((PW, BW), F32)
DIAGONAL = jax.ShapeDtypeStruct((BW, BW), F32)


def call(kernel, ins, outs, name, args):
    return pl.pallas_call(
        kernel,
        in_specs=ins,
        out_specs=[VMEM] * len(outs),
        out_shape=outs,
        compiler_params=params(),
        cost_estimate=cost(10**9, 6 * 10**6),
        name=name,
    )(*args)


def whiten_kernel(moves, *refs):
    n = 4 if moves else 6
    g_refs, diag_refs = refs[:4], refs[4:n]
    first_ref, second_ref, z_ref, y_ref, t_ref, d_ref = refs[-6:]
    z, y, t, d_col, d_row, inv_row, fro = newton(gram_of(g_refs, diag_refs))
    wt = jnp.sqrt(d_col) * z.T * (inv_row / jnp.sqrt(fro))
    first_ref[...] = wt[:BW]
    second_ref[...] = wt[BW:]
    if moves:
        apply_to(wt[BW:], refs[n : n + 2], HALVES, refs[n + 2])
    z_ref[...] = z
    y_ref[...] = y
    t_ref[...] = t
    root = jnp.sqrt(d_col) * jnp.sqrt(d_row)
    d_ref[...] = jnp.concatenate([root[:BW, :BW], root[BW:, BW:]], axis=0)


def whiten(grams, diags, xs=()):
    args = [*grams, *diags, *xs]
    outs = [ROWS_OF_W, ROWS_OF_W, SQUARE, SQUARE, SQUARE, SCALES]
    if xs:
        outs = [BLOCK] + outs
    return call(functools.partial(whiten_kernel, bool(xs)), [VMEM] * len(args), outs, "whiten", args)


def next_diagonals(z_ref, y_ref, t_ref, d_ref):
    ys = split(dot3(split(y_ref[...]), split(t_ref[...])))
    new = dot3(ys, split(z_ref[...]))
    return new[:BW, :BW] * d_ref[:BW], new[BW:, BW:] * d_ref[BW:]


def kept_first_kernel(w_ref, z_ref, y_ref, t_ref, d_ref, x0_ref, x1_ref, kept_ref, diag0_ref, diag1_ref):
    apply_to(w_ref[...], (x0_ref, x1_ref), HALVES, kept_ref)
    diag0_ref[...], diag1_ref[...] = next_diagonals(z_ref, y_ref, t_ref, d_ref)


def kept_first(*args):
    return call(kept_first_kernel, [VMEM] * 7, [BLOCK, DIAGONAL, DIAGONAL], "kept_first", args)


def kept_second_kernel(form, w_ref, z_ref, y_ref, t_ref, d_ref, x0_ref, x1_ref, kept_ref, diag_ref, more_ref):
    apply_to(w_ref[...], (x0_ref, x1_ref), form, kept_ref)
    more_ref[:, :BW], diag_ref[...] = next_diagonals(z_ref, y_ref, t_ref, d_ref)
    more_ref[:, BW:] = w_ref[...]


def kept_second(form, *args):
    more = jax.ShapeDtypeStruct((BW, BW + PW), F32)
    kernel = functools.partial(kept_second_kernel, form)
    return call(kernel, [VMEM] * 7, [BLOCK, DIAGONAL, more], "kept_second", args)


def on_second_core_kernel(form, core_ref, w_ref, x0_ref, x1_ref, out_ref):
    @pl.when(core_ref[0] != 0)
    def _():
        apply_to(w_ref[...], (x0_ref, x1_ref), form, out_ref)


def on_second_core(form, core, w, xs, name):
    kernel = functools.partial(on_second_core_kernel, form)
    return call(kernel, [SMEM] + [VMEM] * 3, [BLOCK], name, [core, w, *xs])[0]


def combine_kernel(form, core_ref, w_ref, s0_ref, s1_ref, other_ref, kept_ref, *refs):
    in_ref, out_ref = refs[-2:]

    @pl.when(core_ref[0] == 0)
    def _():
        in_ref[:, :RH] = other_ref[:, RH:]
        in_ref[:, RH:] = other_ref[:, :RH]

    @pl.when(core_ref[0] != 0)
    def _():
        apply_to(w_ref[...], (s0_ref, s1_ref), form, in_ref)

    total = jnp.zeros((PW, PW), F32)
    for j in range(0, RB, CH):
        a = jnp.concatenate(split(in_ref[:, j : j + CH]), axis=0)
        b = jnp.concatenate(split(kept_ref[:, j : j + CH]), axis=0)
        total += mxu(a, b, NT)
    out_ref[...] = (total[:BW, :BW] + total[BW:, BW:]) + (total[:BW, BW:] + total[BW:, :BW])


def combine(form, core, w, shadow, other, kept):
    kernel = functools.partial(combine_kernel, form)
    args = [core, w, *shadow, other, kept]
    return call(kernel, [SMEM] + [VMEM] * 5, [BLOCK, DIAGONAL], "combine", args)


def by_core(w, even):
    parts = [w[i : i + 32] for i in range(0, PW, 32)]
    evens = jnp.concatenate(parts[0::2], axis=0)
    odds = jnp.concatenate(parts[1::2], axis=0)
    return jnp.where(even, evens, odds)


def last_kernel(core_ref, thr_ref, *refs):
    g_refs, diag_refs, x_refs = refs[:4], refs[4:6], refs[6:8]
    send_ref, w_ref = refs[8:]
    core = core_ref[0]
    z, y, t, d_col, d_row, inv_row, fro = newton(gram_of(g_refs, diag_refs))
    y = dot3(split(y), split(t))
    norm = jnp.sqrt(d_col * jnp.sum(z * y, axis=1, keepdims=True) + 1e-06)
    at_row = lax.broadcasted_iota(jnp.int32, (PW, PW), 0)
    at_col = lax.broadcasted_iota(jnp.int32, (PW, PW), 1)
    thr_row = jnp.where(core == 0, thr_ref[:, :PW], thr_ref[:, PW:])
    thr = jnp.sum(jnp.where(at_row == at_col, thr_row, 0.0), axis=1, keepdims=True)
    factor = jnp.maximum(norm - thr, 0.0) / norm
    wt = (factor * jnp.sqrt(d_col)) * z.T * (inv_row / jnp.sqrt(fro))
    apply_to(by_core(wt, core != 0), x_refs, PLAIN, send_ref, core * RH)
    w_ref[...] = by_core(wt, core == 0)


def last(core, thr, grams, diags, xs):
    return pl.pallas_call(
        last_kernel,
        in_specs=[SMEM] + [VMEM] * 9,
        out_specs=[VMEM] * 2,
        out_shape=[jax.ShapeDtypeStruct((BW, RB), F32), jax.ShapeDtypeStruct((BW, PW), F32)],
        compiler_params=params(),
        cost_estimate=cost(10**9, 6 * 10**6),
        name="last",
    )(core, thr, *grams, *diags, *xs)


def last_kept_kernel(core_ref, w_ref, k_ref, m_ref, got_ref, out_ref):
    core = core_ref[0]
    mine = pl.multiple_of(core * BW, BW)
    apply_to(w_ref[...], (k_ref, m_ref), PLAIN, out_ref.at[pl.ds(mine, BW)], core * RH)
    out_ref[pl.ds(pl.multiple_of(BW - mine, BW), BW)] = got_ref[...]


def last_kept(core, w, xs, got):
    return pl.pallas_call(
        last_kept_kernel,
        in_specs=[SMEM] + [VMEM] * 4,
        out_specs=VMEM,
        out_shape=jax.ShapeDtypeStruct((PW, RB), F32),
        compiler_params=params(),
        cost_estimate=cost(10**9, 6 * 10**6),
        name="last_kept",
    )(core, w, *xs, got)


def to(block, where):
    route = []
    for i in range(8):
        for c in range(2):
            for g in range(8):
                goal = where(i, c, g)
                if goal is not None:
                    ti, tc, tg = goal
                    route.append(((i * 2 + c) * 8 + g, (ti * 2 + tc) * 8 + tg))
    return lax.ppermute(block, AXES, route)


def swap_cores(block):
    return to(block, lambda i, c, g: (i, 1 - c, g))


def onward(block):
    return to(block, lambda i, c, g: (i, 1, g) if c == 0 else (i, 0, (g + 1) % 8))


def backward(block):
    return to(block, lambda i, c, g: (i, 1, (g - 1) % 8) if c == 0 else (i, 0, g))


def behind(block, core):
    return to(block, lambda i, c, g: (i, 1, (g - 1) % 8) if c == core else None)


def beside(block):
    return to(block, lambda i, c, g: (i, 0, g) if c == 1 else None)


def reduced(partial):
    pair = partial + to(partial, lambda i, c, g: (i ^ 1, c, g))
    return [pair] + [to(pair, lambda i, c, g, k=k: (i ^ k, c, g)) for k in (2, 4, 6)]


def on_device(observed, estimate, mask, threshold):
    core = lax.axis_index("core").reshape(1).astype(jnp.int32)
    thr = to(threshold.reshape(1, -1), lambda i, c, g: (i, c, (g - 1) % 8))
    keep, send = fill(core, observed, estimate, mask)
    got = swap_cores(send)
    grams = reduced(gram_second(got, *gram_first(keep)))
    second, w0, _, *rest = whiten(grams, [], (keep, got))
    joined = onward(second)
    first, diag0, diag1 = kept_first(w0, *rest, keep, got)
    shadow, shadow_form = (behind(first, 0), second), SHADOW
    diags = [diag0, onward(diag1)]
    xs, form = (first, joined), CROSSED
    partial = gram_cross(first, joined, shadow[0], thr)
    for round_index in range(1, ROUNDS - 1):
        w0, w1, *rest = whiten(reduced(partial), diags)
        w_shadow = behind(w0, 0)
        given = on_second_core(form, core, w0, xs, "given")
        other = beside(given)
        kept, diag1, more = kept_second(form, w1, *rest, *xs)
        more = backward(more)
        joined, partial = combine(shadow_form, core, w_shadow, shadow, other, kept)
        diags = [more[:, :BW], diag1]
        xs, form = (joined, kept), PLAIN
        if round_index + 2 < ROUNDS:
            moved = on_second_core(shadow_form, core, more[:, BW:], shadow, "shadow")
            shadow, shadow_form = (to(given, lambda i, c, g: (i, 1, (g - 1) % 8) if c == 1 else None), moved), PLAIN
    send, w = last(core, thr, reduced(partial), diags, xs)
    got = swap_cores(send)
    packed = last_kept(core, w, xs, got).reshape(64, 4, RB)
    landed = lax.all_to_all(packed, ("zx", "pairs"), split_axis=0, concat_axis=0, tiled=True)
    landed = landed.reshape(8, 8, 4, RB)
    landed = jnp.roll(landed, 1, axis=1).transpose(2, 1, 0, 3)
    return landed.reshape(32, 8 * RB)


def solution(mesh):
    finer = Mesh(mesh.devices.reshape(8, 2, 8), AXES)
    placed = P(("zx", "core"), "pairs")
    return jax.shard_map(
        on_device,
        mesh=finer,
        in_specs=(placed, placed, placed, P("pairs")),
        out_specs=P(AXES, None),
        check_vma=False,
    )
```

```python
import functools

import jax
import jax.numpy as jnp
from jax import lax
from jax.experimental import pallas as pl
from jax.experimental.pallas import tpu as pltpu
from jax.sharding import Mesh, PartitionSpec as P

BW = 128
PW = 2 * BW
RH = 1536
RB = 2 * RH
CH = 512
AXES = ("zx", "core", "pairs")
F32 = jnp.float32
BF16 = jnp.bfloat16
VMEM = pl.BlockSpec(memory_space=pltpu.VMEM)
ANY = pl.BlockSpec(memory_space=pl.ANY)
SMEM = pl.BlockSpec(memory_space=pltpu.SMEM)
NN = (((1,), (0,)), ((), ()))
NT = (((1,), (1,)), ((), ()))


def params(mib=44):
    return pltpu.CompilerParams(vmem_limit_bytes=mib * 1024 * 1024)


def cost(flops, moved):
    return pl.CostEstimate(flops=flops * 30, bytes_accessed=moved, transcendentals=0)


def split(x):
    high = x.astype(BF16)
    return high, (x - high.astype(F32)).astype(BF16)


def mxu(a, b, dims=NN):
    return lax.dot_general(a, b, dims, preferred_element_type=F32)


def dot3(a, b):
    (ah, al), (bh, bl) = a, b
    return mxu(ah, bh) + (mxu(ah, bl) + mxu(al, bh))


def fill_kernel(core_ref, obs_ref, est_ref, mask_ref, keep_ref, send_ref):
    filled = jnp.where(mask_ref[...] == 1, obs_ref[...], est_ref[...])
    first = core_ref[0] == 0
    a = filled[:, :PW]
    b = filled[:, PW:]
    keep_ref[...] = jnp.where(first, a, b).T
    send_ref[...] = jnp.where(first, b, a).T


def fill(core, observed, estimate, mask):
    step = 256
    rows = pl.BlockSpec((step, 2 * PW), lambda i: (i, 0))
    out = pl.BlockSpec((PW, step), lambda i: (0, i))
    return pl.pallas_call(
        fill_kernel,
        grid=(RH // step,),
        in_specs=[SMEM, rows, rows, rows],
        out_specs=[out, out],
        out_shape=[jax.ShapeDtypeStruct((PW, RH), F32)] * 2,
        compiler_params=params(60),
        cost_estimate=cost(10**6, 15 * 10**6),
        name="fill",
    )(core, observed, estimate, mask)


def gram_parts(x_ref):
    hh = jnp.zeros((PW, PW), F32)
    hl = jnp.zeros((PW, PW), F32)
    for j in range(0, RH, CH):
        h, l = split(x_ref[:, j : j + CH])
        hh += mxu(h, h, NT)
        hl += mxu(h, l, NT)
    return hh, hl


def gram_first_kernel(x_ref, hh_ref, hl_ref):
    hh_ref[...], hl_ref[...] = gram_parts(x_ref)


def gram_second_kernel(x_ref, hh_ref, hl_ref, out_ref):
    hh, hl = gram_parts(x_ref)
    hl += hl_ref[...]
    g = hh + hh_ref[...] + (hl + hl.T)
    at_row = lax.broadcasted_iota(jnp.int32, (BW, BW), 0)
    at_col = lax.broadcasted_iota(jnp.int32, (BW, BW), 1)
    d0, d1 = g[:BW, :BW], g[BW:, BW:]
    out_ref[0:BW] = g[:BW, BW:]
    out_ref[BW : 2 * BW] = jnp.where(at_col > at_row, d0, d1)
    on_diag = jnp.sum(jnp.where(at_col == at_row, d0, 0.0), axis=0, keepdims=True)
    out_ref[2 * BW :] = jnp.broadcast_to(on_diag, (8, BW))


def gram_cross_kernel(k_ref, m_ref, *refs):
    out_ref = refs[-1]
    total = jnp.zeros((PW, PW), F32)
    for half in range(2):
        for j in range(0, RH, CH):
            ka = half * RH + j
            ma = (1 - half) * RH + j
            k = jnp.concatenate(split(k_ref[:, ka : ka + CH]), axis=0)
            m = jnp.concatenate(split(m_ref[:, ma : ma + CH]), axis=0)
            total += mxu(k, m, NT)
    out_ref[...] = (total[:BW, :BW] + total[BW:, BW:]) + (total[:BW, BW:] + total[BW:, :BW])


def gram_first(x):
    return pl.pallas_call(
        gram_first_kernel,
        in_specs=[VMEM],
        out_specs=[VMEM] * 2,
        out_shape=[jax.ShapeDtypeStruct((PW, PW), F32)] * 2,
        compiler_params=params(),
        cost_estimate=cost(4 * RH * PW * PW, 3 * 10**6),
        name="gram_first",
    )(x)


def gram_second(x, hh, hl):
    return pl.pallas_call(
        gram_second_kernel,
        in_specs=[VMEM] * 3,
        out_specs=VMEM,
        out_shape=jax.ShapeDtypeStruct((2 * BW + 8, BW), F32),
        compiler_params=params(),
        cost_estimate=cost(4 * RH * PW * PW, 3 * 10**6),
        name="gram_second",
    )(x, hh, hl)


def gram_cross(k, m, *arrived):
    return pl.pallas_call(
        gram_cross_kernel,
        in_specs=[VMEM] * 2 + [ANY] * len(arrived),
        out_specs=VMEM,
        out_shape=jax.ShapeDtypeStruct((BW, BW), F32),
        compiler_params=params(),
        cost_estimate=cost(4 * RH * PW * PW, 3 * 10**6),
        name="gram_cross",
    )(k, m, *arrived)


def newton(gram):
    at_row = lax.broadcasted_iota(jnp.int32, (PW, PW), 0)
    at_col = lax.broadcasted_iota(jnp.int32, (PW, PW), 1)
    on = at_row == at_col
    diag = jnp.where(on, gram, 0.0)
    d_col = jnp.sum(diag, axis=1, keepdims=True) + 1e-06
    d_row = jnp.sum(diag, axis=0, keepdims=True) + 1e-06
    inv_col = 1.0 / jnp.sqrt(d_col)
    inv_row = 1.0 / jnp.sqrt(d_row)
    normed = gram * inv_col * inv_row
    fro = jnp.sqrt(jnp.sum(jnp.sum(normed * normed, axis=1, keepdims=True), axis=0, keepdims=True))
    y = normed / fro
    three = jnp.where(on, 1.5, 0.0)
    t = three - 0.5 * y
    ts = split(t)
    y = dot3(split(y), ts)
    z, zs = t, ts
    ys = split(y)
    t = three - 0.5 * dot3(zs, ys)
    ts = split(t)
    y = dot3(ys, ts)
    z = dot3(ts, zs)
    ys, zs = split(y), split(z)
    t = three - 0.5 * dot3(zs, ys)
    ts = split(t)
    z = dot3(ts, zs)
    return z, y, t, d_col, d_row, inv_row, fro


def gram_of(g_refs, diag_refs):
    total = (g_refs[0][...] + g_refs[1][...]) + (g_refs[2][...] + g_refs[3][...])
    if diag_refs:
        d0, cross, d1 = diag_refs[0][...], total, diag_refs[1][...]
    else:
        cross, both, on_diag = total[:BW], total[BW : 2 * BW], total[2 * BW : 2 * BW + 1]
        at_row = lax.broadcasted_iota(jnp.int32, (BW, BW), 0)
        at_col = lax.broadcasted_iota(jnp.int32, (BW, BW), 1)
        turned = both.T
        d0 = jnp.where(at_col == at_row, on_diag, jnp.where(at_col > at_row, both, turned))
        d1 = jnp.where(at_col > at_row, turned, both)
    top = jnp.concatenate([d0, cross], axis=1)
    bottom = jnp.concatenate([cross.T, d1], axis=1)
    return jnp.concatenate([top, bottom], axis=0)


HALVES = "halves"
CROSSED = (False, True)
SHADOW = (True, False)
PLAIN = (False, False)


PIECES = (RB,)


def rows_of(x_ref, at):
    if isinstance(x_ref, list):
        for piece in x_ref:
            if at < piece.shape[1]:
                return piece[:, at : at + CH]
            at -= piece.shape[1]
    return x_ref[:, at : at + CH]


def columns(x_refs, form, half, j):
    if form == HALVES:
        return x_refs[half][:, j : j + CH]
    ats = [((1 - half) if crossed else half) * RH + j for crossed in form]
    return jnp.concatenate([rows_of(x_ref, at) for x_ref, at in zip(x_refs, ats)], axis=0)


def apply_to(w, x_refs, form, out_ref, offset=None):
    wh, wl = split(w)
    both = jnp.concatenate([wh, wl], axis=0)
    for half in range(2):
        for j in range(0, RH, CH):
            xh, xl = split(columns(x_refs, form, half, j))
            wide = mxu(both, xh)
            value = wide[:BW] + (wide[BW:] + mxu(wh, xl))
            if offset is None:
                out_ref[:, half * RH + j : half * RH + j + CH] = value
            else:
                at = pl.multiple_of((offset if half == 0 else RH - offset) + j, 128)
                out_ref[:, pl.ds(at, CH)] = value


BLOCK = jax.ShapeDtypeStruct((BW, RB), F32)
ROWS_OF_W = jax.ShapeDtypeStruct((BW, PW), F32)
SQUARE = jax.ShapeDtypeStruct((PW, PW), F32)
SCALES = jax.ShapeDtypeStruct((PW, BW), F32)
DIAGONAL = jax.ShapeDtypeStruct((BW, BW), F32)


def call(kernel, ins, outs, name, args):
    return pl.pallas_call(
        kernel,
        in_specs=ins,
        out_specs=[VMEM] * len(outs),
        out_shape=outs,
        compiler_params=params(),
        cost_estimate=cost(10**9, 6 * 10**6),
        name=name,
    )(*args)


def whiten_kernel(first_round, *refs):
    n = 4 if first_round else 6
    g_refs, diag_refs = refs[:4], refs[4:n]
    first_ref, second_ref, z_ref, y_ref, t_ref, d_ref = refs[-6:]
    z, y, t, d_col, d_row, inv_row, fro = newton(gram_of(g_refs, diag_refs))
    wt = jnp.sqrt(d_col) * z.T * (inv_row / jnp.sqrt(fro))
    if first_round:
        apply_to(wt[BW:], refs[n : n + 2], HALVES, second_ref)
        apply_to(wt[:BW], refs[n : n + 2], HALVES, first_ref)
    else:
        first_ref[...] = wt[:BW]
        second_ref[...] = wt[BW:]
    z_ref[...] = z
    y_ref[...] = y
    t_ref[...] = t
    root = jnp.sqrt(d_col) * jnp.sqrt(d_row)
    d_ref[...] = jnp.concatenate([root[:BW, :BW], root[BW:, BW:]], axis=0)


def whiten(grams, diags, xs=(), arrived=()):
    args = [*grams, *diags, *xs, *arrived]
    ins = [VMEM] * (len(args) - len(arrived)) + [ANY] * len(arrived)
    outs = [BLOCK if xs else ROWS_OF_W] * 2 + [SQUARE, SQUARE, SQUARE, SCALES]
    return call(functools.partial(whiten_kernel, bool(xs)), ins, outs, "whiten", args)


def next_diagonals(z_ref, y_ref, t_ref, d_ref):
    ys = split(dot3(split(y_ref[...]), split(t_ref[...])))
    new = dot3(ys, split(z_ref[...]))
    return new[:BW, :BW] * d_ref[:BW], new[BW:, BW:] * d_ref[BW:]


def diagonals_kernel(z_ref, y_ref, t_ref, d_ref, diag0_ref, diag1_ref):
    diag0_ref[...], diag1_ref[...] = next_diagonals(z_ref, y_ref, t_ref, d_ref)


def diagonals(*args):
    return call(diagonals_kernel, [VMEM] * 4, [DIAGONAL, DIAGONAL], "diagonals", args)


def kept_second_kernel(form, w_ref, z_ref, y_ref, t_ref, d_ref, x0_ref, x1_ref, kept_ref, diag_ref, more_ref):
    apply_to(w_ref[...], (x0_ref, x1_ref), form, kept_ref)
    more_ref[:, :BW], diag_ref[...] = next_diagonals(z_ref, y_ref, t_ref, d_ref)
    more_ref[:, BW:] = w_ref[...]


def kept_second(form, *args):
    more = jax.ShapeDtypeStruct((BW, BW + PW), F32)
    kernel = functools.partial(kept_second_kernel, form)
    return call(kernel, [VMEM] * 7, [BLOCK, DIAGONAL, more], "kept_second", args)


def on_second_core_kernel(form, core_ref, w_ref, x0_ref, x1_ref, out_ref, *piece_refs):
    @pl.when(core_ref[0] != 0)
    def _():
        apply_to(w_ref[...], (x0_ref, x1_ref), form, out_ref)
        at = 0
        for piece_ref in piece_refs:
            piece_ref[...] = out_ref[:, at : at + piece_ref.shape[1]]
            at += piece_ref.shape[1]


def on_second_core(form, core, w, xs, name, pieces=()):
    kernel = functools.partial(on_second_core_kernel, form)
    outs = [BLOCK] + [jax.ShapeDtypeStruct((BW, piece), F32) for piece in pieces]
    return call(kernel, [SMEM] + [VMEM] * 3, outs, name, [core, w, *xs])


def combine_kernel(form, n, core_ref, w_ref, *refs):
    s0_ref = list(refs[:n])
    s1_ref, other_ref, kept_ref = refs[n : n + 3]
    in_ref, out_ref = refs[-2:]

    @pl.when(core_ref[0] == 0)
    def _():
        in_ref[:, :RH] = other_ref[:, RH:]
        in_ref[:, RH:] = other_ref[:, :RH]

    @pl.when(core_ref[0] != 0)
    def _():
        apply_to(w_ref[...], (s0_ref, s1_ref), form, in_ref)

    total = jnp.zeros((PW, PW), F32)
    for j in range(0, RB, CH):
        a = jnp.concatenate(split(in_ref[:, j : j + CH]), axis=0)
        b = jnp.concatenate(split(kept_ref[:, j : j + CH]), axis=0)
        total += mxu(a, b, NT)
    out_ref[...] = (total[:BW, :BW] + total[BW:, BW:]) + (total[:BW, BW:] + total[BW:, :BW])


def combine(form, core, w, shadow, other, kept, *arrived):
    pieces, second = shadow
    kernel = functools.partial(combine_kernel, form, len(pieces))
    args = [core, w, *pieces, second, other, kept, *arrived]
    ins = [SMEM] + [VMEM] * (len(pieces) + 4) + [ANY] * len(arrived)
    return call(kernel, ins, [BLOCK, DIAGONAL], "combine", args)


def by_core(w, even):
    parts = [w[i : i + 32] for i in range(0, PW, 32)]
    evens = jnp.concatenate(parts[0::2], axis=0)
    odds = jnp.concatenate(parts[1::2], axis=0)
    return jnp.where(even, evens, odds)


def last_kernel(core_ref, thr_ref, *refs):
    g_refs, diag_refs, x_refs = refs[:4], refs[4:6], refs[6:8]
    send_ref, w_ref = refs[8:]
    core = core_ref[0]
    z, y, t, d_col, d_row, inv_row, fro = newton(gram_of(g_refs, diag_refs))
    y = dot3(split(y), split(t))
    norm = jnp.sqrt(d_col * jnp.sum(z * y, axis=1, keepdims=True) + 1e-06)
    at_row = lax.broadcasted_iota(jnp.int32, (PW, PW), 0)
    at_col = lax.broadcasted_iota(jnp.int32, (PW, PW), 1)
    thr_row = jnp.where(core == 0, thr_ref[:, :PW], thr_ref[:, PW:])
    thr = jnp.sum(jnp.where(at_row == at_col, thr_row, 0.0), axis=1, keepdims=True)
    factor = jnp.maximum(norm - thr, 0.0) / norm
    wt = (factor * jnp.sqrt(d_col)) * z.T * (inv_row / jnp.sqrt(fro))
    apply_to(by_core(wt, core != 0), x_refs, PLAIN, send_ref, core * RH)
    w_ref[...] = by_core(wt, core == 0)


def last(core, thr, grams, diags, xs):
    return pl.pallas_call(
        last_kernel,
        in_specs=[SMEM] + [VMEM] * 9,
        out_specs=[VMEM] * 2,
        out_shape=[jax.ShapeDtypeStruct((BW, RB), F32), jax.ShapeDtypeStruct((BW, PW), F32)],
        compiler_params=params(),
        cost_estimate=cost(10**9, 6 * 10**6),
        name="last",
    )(core, thr, *grams, *diags, *xs)


def last_kept_kernel(core_ref, w_ref, k_ref, m_ref, got_ref, out_ref):
    core = core_ref[0]
    mine = pl.multiple_of(core * BW, BW)
    apply_to(w_ref[...], (k_ref, m_ref), PLAIN, out_ref.at[pl.ds(mine, BW)], core * RH)
    out_ref[pl.ds(pl.multiple_of(BW - mine, BW), BW)] = got_ref[...]


def last_kept(core, w, xs, got):
    return pl.pallas_call(
        last_kept_kernel,
        in_specs=[SMEM] + [VMEM] * 4,
        out_specs=VMEM,
        out_shape=jax.ShapeDtypeStruct((PW, RB), F32),
        compiler_params=params(),
        cost_estimate=cost(10**9, 6 * 10**6),
        name="last_kept",
    )(core, w, *xs, got)


def to(block, where):
    route = []
    for i in range(8):
        for c in range(2):
            for g in range(8):
                goal = where(i, c, g)
                if goal is not None:
                    ti, tc, tg = goal
                    route.append(((i * 2 + c) * 8 + g, (ti * 2 + tc) * 8 + tg))
    return lax.ppermute(block, AXES, route)


def swap_cores(block):
    return to(block, lambda i, c, g: (i, 1 - c, g))


def onward(block):
    return to(block, lambda i, c, g: (i, 1, g) if c == 0 else (i, 0, (g + 1) % 8))


def backward(block):
    return to(block, lambda i, c, g: (i, 1, (g - 1) % 8) if c == 0 else (i, 0, g))


def behind(block, core):
    return to(block, lambda i, c, g: (i, 1, (g - 1) % 8) if c == core else None)


def beside(block):
    return to(block, lambda i, c, g: (i, 0, g) if c == 1 else None)


def reduced(partial):
    pair = partial + to(partial, lambda i, c, g: (i ^ 1, c, g))
    return [pair] + [to(pair, lambda i, c, g, k=k: (i ^ k, c, g)) for k in (2, 4, 6)]


def on_device(observed, estimate, mask, threshold):
    core = lax.axis_index("core").reshape(1).astype(jnp.int32)
    thr = to(threshold.reshape(1, -1), lambda i, c, g: (i, c, (g - 1) % 8))
    keep, send = fill(core, observed, estimate, mask)
    got = swap_cores(send)
    grams = reduced(gram_second(got, *gram_first(keep)))
    first, second, *rest = whiten(grams, [], (keep, got))
    joined = onward(second)
    back = behind(first, 0)
    diag0, diag1 = diagonals(*rest)
    diags = [diag0, onward(diag1)]
    partial = gram_cross(first, joined, back, thr)
    xs = (first, joined)
    w0, w1, *rest = whiten(reduced(partial), diags)
    w_shadow = behind(w0, 0)
    (given,) = on_second_core(CROSSED, core, w0, xs, "given")
    other = beside(given)
    pieces = [behind(given, 1)]
    kept, diag1, more = kept_second(CROSSED, w1, *rest, *xs)
    more = backward(more)
    joined, partial = combine(SHADOW, core, w_shadow, ([back], second), other, kept)
    (moved,) = on_second_core(SHADOW, core, more[:, BW:], (back, second), "shadow")
    diags = [more[:, :BW], diag1]
    xs = (joined, kept)
    w0, w1, *rest = whiten(reduced(partial), diags)
    w_shadow = behind(w0, 0)
    (given,) = on_second_core(PLAIN, core, w0, xs, "given")
    other = beside(given)
    kept, diag1, more = kept_second(PLAIN, w1, *rest, *xs)
    more = backward(more)
    joined, partial = combine(PLAIN, core, w_shadow, (pieces, moved), other, kept)
    diags = [more[:, :BW], diag1]
    xs = (joined, kept)
    send, w = last(core, thr, reduced(partial), diags, xs)
    got = swap_cores(send)
    packed = last_kept(core, w, xs, got).reshape(64, 4, RB)
    landed = lax.all_to_all(packed, ("zx", "pairs"), split_axis=0, concat_axis=0, tiled=True)
    landed = landed.reshape(8, 8, 4, RB)
    landed = jnp.roll(landed, 1, axis=1).transpose(2, 1, 0, 3)
    return landed.reshape(32, 8 * RB)


def solution(mesh):
    finer = Mesh(mesh.devices.reshape(8, 2, 8), AXES)
    placed = P(("zx", "core"), "pairs")
    return jax.shard_map(
        on_device,
        mesh=finer,
        in_specs=(placed, placed, placed, P("pairs")),
        out_specs=P(AXES, None),
        check_vma=False,
    )
```

```python
import functools

import jax
import jax.numpy as jnp
from jax import lax
from jax.experimental import pallas as pl
from jax.experimental.pallas import tpu as pltpu
from jax.sharding import Mesh, PartitionSpec as P

BW = 128
PW = 2 * BW
RH = 1536
RB = 2 * RH
CH = 512
AXES = ("zx", "core", "pairs")
F32 = jnp.float32
BF16 = jnp.bfloat16
VMEM = pl.BlockSpec(memory_space=pltpu.VMEM)
ANY = pl.BlockSpec(memory_space=pl.ANY)
SMEM = pl.BlockSpec(memory_space=pltpu.SMEM)
NN = (((1,), (0,)), ((), ()))
NT = (((1,), (1,)), ((), ()))


def params(mib=44):
    return pltpu.CompilerParams(vmem_limit_bytes=mib * 1024 * 1024)


def cost(flops, moved):
    return pl.CostEstimate(flops=flops * 30, bytes_accessed=moved, transcendentals=0)


def split(x):
    high = x.astype(BF16)
    return high, (x - high.astype(F32)).astype(BF16)


def mxu(a, b, dims=NN):
    return lax.dot_general(a, b, dims, preferred_element_type=F32)


def dot3(a, b):
    (ah, al), (bh, bl) = a, b
    return mxu(ah, bh) + (mxu(ah, bl) + mxu(al, bh))


def fill_kernel(core_ref, obs_ref, est_ref, mask_ref, keep_ref, send_ref):
    filled = jnp.where(mask_ref[...] == 1, obs_ref[...], est_ref[...])
    first = core_ref[0] == 0
    a = filled[:, :PW]
    b = filled[:, PW:]
    keep_ref[...] = jnp.where(first, a, b).T
    send_ref[...] = jnp.where(first, b, a).T


def fill(core, observed, estimate, mask):
    step = 512
    rows = pl.BlockSpec((step, 2 * PW), lambda i: (i, 0))
    out = pl.BlockSpec((PW, step), lambda i: (0, i))
    return pl.pallas_call(
        fill_kernel,
        grid=(RH // step,),
        in_specs=[SMEM, rows, rows, rows],
        out_specs=[out, out],
        out_shape=[jax.ShapeDtypeStruct((PW, RH), F32)] * 2,
        compiler_params=params(50),
        cost_estimate=cost(10**6, 15 * 10**6),
        name="fill",
    )(core, observed, estimate, mask)


def gram_parts(x_ref):
    hh = jnp.zeros((PW, PW), F32)
    hl = jnp.zeros((PW, PW), F32)
    for j in range(0, RH, CH):
        h, l = split(x_ref[:, j : j + CH])
        hh += mxu(h, h, NT)
        hl += mxu(h, l, NT)
    return hh, hl


def gram_first_kernel(x_ref, hh_ref, hl_ref):
    hh_ref[...], hl_ref[...] = gram_parts(x_ref)


def gram_second_kernel(x_ref, hh_ref, hl_ref, out_ref):
    hh, hl = gram_parts(x_ref)
    hl += hl_ref[...]
    g = hh + hh_ref[...] + (hl + hl.T)
    at_row = lax.broadcasted_iota(jnp.int32, (BW, BW), 0)
    at_col = lax.broadcasted_iota(jnp.int32, (BW, BW), 1)
    d0, d1 = g[:BW, :BW], g[BW:, BW:]
    out_ref[0:BW] = g[:BW, BW:]
    out_ref[BW : 2 * BW] = jnp.where(at_col > at_row, d0, d1)
    on_diag = jnp.sum(jnp.where(at_col == at_row, d0, 0.0), axis=0, keepdims=True)
    out_ref[2 * BW :] = jnp.broadcast_to(on_diag, (8, BW))


def gram_cross_kernel(k_ref, m_ref, *refs):
    out_ref = refs[-1]
    total = jnp.zeros((PW, PW), F32)
    for half in range(2):
        for j in range(0, RH, CH):
            ka = half * RH + j
            ma = (1 - half) * RH + j
            k = jnp.concatenate(split(k_ref[:, ka : ka + CH]), axis=0)
            m = jnp.concatenate(split(m_ref[:, ma : ma + CH]), axis=0)
            total += mxu(k, m, NT)
    out_ref[...] = (total[:BW, :BW] + total[BW:, BW:]) + (total[:BW, BW:] + total[BW:, :BW])


def gram_first(x):
    return pl.pallas_call(
        gram_first_kernel,
        in_specs=[VMEM],
        out_specs=[VMEM] * 2,
        out_shape=[jax.ShapeDtypeStruct((PW, PW), F32)] * 2,
        compiler_params=params(),
        cost_estimate=cost(4 * RH * PW * PW, 3 * 10**6),
        name="gram_first",
    )(x)


def gram_second(x, hh, hl):
    return pl.pallas_call(
        gram_second_kernel,
        in_specs=[VMEM] * 3,
        out_specs=VMEM,
        out_shape=jax.ShapeDtypeStruct((2 * BW + 8, BW), F32),
        compiler_params=params(),
        cost_estimate=cost(4 * RH * PW * PW, 3 * 10**6),
        name="gram_second",
    )(x, hh, hl)


def gram_cross(k, m, *arrived):
    return pl.pallas_call(
        gram_cross_kernel,
        in_specs=[VMEM] * 2 + [ANY] * len(arrived),
        out_specs=VMEM,
        out_shape=jax.ShapeDtypeStruct((BW, BW), F32),
        compiler_params=params(),
        cost_estimate=cost(4 * RH * PW * PW, 3 * 10**6),
        name="gram_cross",
    )(k, m, *arrived)


def newton(gram):
    at_row = lax.broadcasted_iota(jnp.int32, (PW, PW), 0)
    at_col = lax.broadcasted_iota(jnp.int32, (PW, PW), 1)
    on = at_row == at_col
    diag = jnp.where(on, gram, 0.0)
    d_col = jnp.sum(diag, axis=1, keepdims=True) + 1e-06
    d_row = jnp.sum(diag, axis=0, keepdims=True) + 1e-06
    inv_col = 1.0 / jnp.sqrt(d_col)
    inv_row = 1.0 / jnp.sqrt(d_row)
    normed = gram * inv_col * inv_row
    fro = jnp.sqrt(jnp.sum(jnp.sum(normed * normed, axis=1, keepdims=True), axis=0, keepdims=True))
    y = normed / fro
    three = jnp.where(on, 1.5, 0.0)
    t = three - 0.5 * y
    ts = split(t)
    y = dot3(split(y), ts)
    z, zs = t, ts
    ys = split(y)
    t = three - 0.5 * dot3(zs, ys)
    ts = split(t)
    y = dot3(ys, ts)
    z = dot3(ts, zs)
    ys, zs = split(y), split(z)
    t = three - 0.5 * dot3(zs, ys)
    ts = split(t)
    z = dot3(ts, zs)
    return z, y, t, d_col, d_row, inv_row, fro


def gram_of(g_refs, diag_refs):
    total = (g_refs[0][...] + g_refs[1][...]) + (g_refs[2][...] + g_refs[3][...])
    if diag_refs:
        d0, cross, d1 = diag_refs[0][...], total, diag_refs[1][...]
    else:
        cross, both, on_diag = total[:BW], total[BW : 2 * BW], total[2 * BW : 2 * BW + 1]
        at_row = lax.broadcasted_iota(jnp.int32, (BW, BW), 0)
        at_col = lax.broadcasted_iota(jnp.int32, (BW, BW), 1)
        turned = both.T
        d0 = jnp.where(at_col == at_row, on_diag, jnp.where(at_col > at_row, both, turned))
        d1 = jnp.where(at_col > at_row, turned, both)
    top = jnp.concatenate([d0, cross], axis=1)
    bottom = jnp.concatenate([cross.T, d1], axis=1)
    return jnp.concatenate([top, bottom], axis=0)


HALVES = "halves"
CROSSED = (False, True)
SHADOW = (True, False)
PLAIN = (False, False)


PIECES = (RB,)


def rows_of(x_ref, at):
    if isinstance(x_ref, list):
        for piece in x_ref:
            if at < piece.shape[1]:
                return piece[:, at : at + CH]
            at -= piece.shape[1]
    return x_ref[:, at : at + CH]


def columns(x_refs, form, half, j):
    if form == HALVES:
        return x_refs[half][:, j : j + CH]
    ats = [((1 - half) if crossed else half) * RH + j for crossed in form]
    return jnp.concatenate([rows_of(x_ref, at) for x_ref, at in zip(x_refs, ats)], axis=0)


def apply_to(w, x_refs, form, out_ref, offset=None):
    wh, wl = split(w)
    both = jnp.concatenate([wh, wl], axis=0)
    for half in range(2):
        for j in range(0, RH, CH):
            xh, xl = split(columns(x_refs, form, half, j))
            wide = mxu(both, xh)
            value = wide[:BW] + (wide[BW:] + mxu(wh, xl))
            if offset is None:
                out_ref[:, half * RH + j : half * RH + j + CH] = value
            else:
                at = pl.multiple_of((offset if half == 0 else RH - offset) + j, 128)
                out_ref[:, pl.ds(at, CH)] = value


BLOCK = jax.ShapeDtypeStruct((BW, RB), F32)
ROWS_OF_W = jax.ShapeDtypeStruct((BW, PW), F32)
SQUARE = jax.ShapeDtypeStruct((PW, PW), F32)
SCALES = jax.ShapeDtypeStruct((PW, BW), F32)
DIAGONAL = jax.ShapeDtypeStruct((BW, BW), F32)


def call(kernel, ins, outs, name, args):
    return pl.pallas_call(
        kernel,
        in_specs=ins,
        out_specs=[VMEM] * len(outs),
        out_shape=outs,
        compiler_params=params(),
        cost_estimate=cost(10**9, 6 * 10**6),
        name=name,
    )(*args)


def whiten_kernel(first_round, *refs):
    n = 4 if first_round else 6
    g_refs, diag_refs = refs[:4], refs[4:n]
    first_ref, second_ref, z_ref, y_ref, t_ref, d_ref = refs[-6:]
    z, y, t, d_col, d_row, inv_row, fro = newton(gram_of(g_refs, diag_refs))
    wt = jnp.sqrt(d_col) * z.T * (inv_row / jnp.sqrt(fro))
    if first_round:
        apply_to(wt[BW:], refs[n : n + 2], HALVES, second_ref)
        apply_to(wt[:BW], refs[n : n + 2], HALVES, first_ref)
    else:
        first_ref[...] = wt[:BW]
        second_ref[...] = wt[BW:]
    z_ref[...] = z
    y_ref[...] = y
    t_ref[...] = t
    root = jnp.sqrt(d_col) * jnp.sqrt(d_row)
    d_ref[...] = jnp.concatenate([root[:BW, :BW], root[BW:, BW:]], axis=0)


def whiten(grams, diags, xs=(), arrived=()):
    args = [*grams, *diags, *xs, *arrived]
    ins = [VMEM] * (len(args) - len(arrived)) + [ANY] * len(arrived)
    outs = [BLOCK if xs else ROWS_OF_W] * 2 + [SQUARE, SQUARE, SQUARE, SCALES]
    return call(functools.partial(whiten_kernel, bool(xs)), ins, outs, "whiten", args)


def next_diagonals(z_ref, y_ref, t_ref, d_ref):
    ys = split(dot3(split(y_ref[...]), split(t_ref[...])))
    new = dot3(ys, split(z_ref[...]))
    return new[:BW, :BW] * d_ref[:BW], new[BW:, BW:] * d_ref[BW:]


def diagonals_kernel(z_ref, y_ref, t_ref, d_ref, diag0_ref, diag1_ref):
    diag0_ref[...], diag1_ref[...] = next_diagonals(z_ref, y_ref, t_ref, d_ref)


def diagonals(*args):
    return call(diagonals_kernel, [VMEM] * 4, [DIAGONAL, DIAGONAL], "diagonals", args)


def kept_second_kernel(form, w_ref, z_ref, y_ref, t_ref, d_ref, x0_ref, x1_ref, kept_ref, diag_ref, more_ref):
    apply_to(w_ref[...], (x0_ref, x1_ref), form, kept_ref)
    more_ref[:, :BW], diag_ref[...] = next_diagonals(z_ref, y_ref, t_ref, d_ref)
    more_ref[:, BW:] = w_ref[...]


def kept_second(form, *args):
    more = jax.ShapeDtypeStruct((BW, BW + PW), F32)
    kernel = functools.partial(kept_second_kernel, form)
    return call(kernel, [VMEM] * 7, [BLOCK, DIAGONAL, more], "kept_second", args)


def on_second_core_kernel(form, core_ref, w_ref, x0_ref, x1_ref, out_ref, *piece_refs):
    @pl.when(core_ref[0] != 0)
    def _():
        apply_to(w_ref[...], (x0_ref, x1_ref), form, out_ref)
        at = 0
        for piece_ref in piece_refs:
            piece_ref[...] = out_ref[:, at : at + piece_ref.shape[1]]
            at += piece_ref.shape[1]


def on_second_core(form, core, w, xs, name, pieces=()):
    kernel = functools.partial(on_second_core_kernel, form)
    outs = [BLOCK] + [jax.ShapeDtypeStruct((BW, piece), F32) for piece in pieces]
    return call(kernel, [SMEM] + [VMEM] * 3, outs, name, [core, w, *xs])


def combine_kernel(form, n, core_ref, w_ref, *refs):
    s0_ref = list(refs[:n])
    s1_ref, other_ref, kept_ref = refs[n : n + 3]
    in_ref, out_ref = refs[-2:]

    @pl.when(core_ref[0] == 0)
    def _():
        in_ref[:, :RH] = other_ref[:, RH:]
        in_ref[:, RH:] = other_ref[:, :RH]

    @pl.when(core_ref[0] != 0)
    def _():
        apply_to(w_ref[...], (s0_ref, s1_ref), form, in_ref)

    total = jnp.zeros((PW, PW), F32)
    for j in range(0, RB, CH):
        a = jnp.concatenate(split(in_ref[:, j : j + CH]), axis=0)
        b = jnp.concatenate(split(kept_ref[:, j : j + CH]), axis=0)
        total += mxu(a, b, NT)
    out_ref[...] = (total[:BW, :BW] + total[BW:, BW:]) + (total[:BW, BW:] + total[BW:, :BW])


def combine(form, core, w, shadow, other, kept, *arrived):
    pieces, second = shadow
    kernel = functools.partial(combine_kernel, form, len(pieces))
    args = [core, w, *pieces, second, other, kept, *arrived]
    ins = [SMEM] + [VMEM] * (len(pieces) + 4) + [ANY] * len(arrived)
    return call(kernel, ins, [BLOCK, DIAGONAL], "combine", args)


def by_core(w, even):
    parts = [w[i : i + 32] for i in range(0, PW, 32)]
    evens = jnp.concatenate(parts[0::2], axis=0)
    odds = jnp.concatenate(parts[1::2], axis=0)
    return jnp.where(even, evens, odds)


def last_kernel(core_ref, thr_ref, *refs):
    g_refs, diag_refs, x_refs = refs[:4], refs[4:6], refs[6:8]
    send_ref, w_ref = refs[8:]
    core = core_ref[0]
    z, y, t, d_col, d_row, inv_row, fro = newton(gram_of(g_refs, diag_refs))
    y = dot3(split(y), split(t))
    norm = jnp.sqrt(d_col * jnp.sum(z * y, axis=1, keepdims=True) + 1e-06)
    at_row = lax.broadcasted_iota(jnp.int32, (PW, PW), 0)
    at_col = lax.broadcasted_iota(jnp.int32, (PW, PW), 1)
    thr_row = jnp.where(core == 0, thr_ref[:, :PW], thr_ref[:, PW:])
    thr = jnp.sum(jnp.where(at_row == at_col, thr_row, 0.0), axis=1, keepdims=True)
    factor = jnp.maximum(norm - thr, 0.0) / norm
    wt = (factor * jnp.sqrt(d_col)) * z.T * (inv_row / jnp.sqrt(fro))
    apply_to(by_core(wt, core != 0), x_refs, PLAIN, send_ref, core * RH)
    w_ref[...] = by_core(wt, core == 0)


def last(core, thr, grams, diags, xs):
    return pl.pallas_call(
        last_kernel,
        in_specs=[SMEM] + [VMEM] * 9,
        out_specs=[VMEM] * 2,
        out_shape=[jax.ShapeDtypeStruct((BW, RB), F32), jax.ShapeDtypeStruct((BW, PW), F32)],
        compiler_params=params(),
        cost_estimate=cost(10**9, 6 * 10**6),
        name="last",
    )(core, thr, *grams, *diags, *xs)


def last_kept_kernel(core_ref, w_ref, k_ref, m_ref, got_ref, out_ref):
    core = core_ref[0]
    wh, wl = split(w_ref[...])
    both = jnp.concatenate([wh, wl], axis=0)
    mine, other = core * 32, 32 - core * 32
    for half in range(2):
        for j in range(0, RH, CH):
            xh, xl = split(columns((k_ref, m_ref), PLAIN, half, j))
            wide = mxu(both, xh)
            value = wide[:BW] + (wide[BW:] + mxu(wh, xl))
            at = pl.multiple_of((core * RH if half == 0 else RH - core * RH) + j, 128)
            for d in range(32):
                out_ref[mine + d, :, pl.ds(at, CH)] = value[4 * d : 4 * d + 4]
    for j in range(0, RB, CH):
        for d in range(32):
            out_ref[other + d, :, j : j + CH] = got_ref[4 * d : 4 * d + 4, j : j + CH]


def last_kept(core, w, xs, got):
    return pl.pallas_call(
        last_kept_kernel,
        in_specs=[SMEM] + [VMEM] * 4,
        out_specs=VMEM,
        out_shape=jax.ShapeDtypeStruct((64, 4, RB), F32),
        compiler_params=params(),
        cost_estimate=cost(10**9, 6 * 10**6),
        name="last_kept",
    )(core, w, *xs, got)


def to(block, where):
    route = []
    for i in range(8):
        for c in range(2):
            for g in range(8):
                goal = where(i, c, g)
                if goal is not None:
                    ti, tc, tg = goal
                    route.append(((i * 2 + c) * 8 + g, (ti * 2 + tc) * 8 + tg))
    return lax.ppermute(block, AXES, route)


def swap_cores(block):
    return to(block, lambda i, c, g: (i, 1 - c, g))


def onward(block):
    return to(block, lambda i, c, g: (i, 1, g) if c == 0 else (i, 0, (g + 1) % 8))


def backward(block):
    return to(block, lambda i, c, g: (i, 1, (g - 1) % 8) if c == 0 else (i, 0, g))


def behind(block, core):
    return to(block, lambda i, c, g: (i, 1, (g - 1) % 8) if c == core else None)


def beside(block):
    return to(block, lambda i, c, g: (i, 0, g) if c == 1 else None)


def reduced(partial):
    pair = partial + to(partial, lambda i, c, g: (i ^ 1, c, g))
    return [pair] + [to(pair, lambda i, c, g, k=k: (i ^ k, c, g)) for k in (2, 4, 6)]


def on_device(observed, estimate, mask, threshold):
    core = lax.axis_index("core").reshape(1).astype(jnp.int32)
    thr = to(threshold.reshape(1, -1), lambda i, c, g: (i, c, (g - 1) % 8))
    keep, send = fill(core, observed, estimate, mask)
    got = swap_cores(send)
    grams = reduced(gram_second(got, *gram_first(keep)))
    first, second, *rest = whiten(grams, [], (keep, got))
    joined = onward(second)
    back = behind(first, 0)
    diag0, diag1 = diagonals(*rest)
    diags = [diag0, onward(diag1)]
    partial = gram_cross(first, joined, back, thr)
    xs = (first, joined)
    w0, w1, *rest = whiten(reduced(partial), diags)
    w_shadow = behind(w0, 0)
    (given,) = on_second_core(CROSSED, core, w0, xs, "given")
    other = beside(given)
    pieces = [behind(given, 1)]
    kept, diag1, more = kept_second(CROSSED, w1, *rest, *xs)
    more = backward(more)
    joined, partial = combine(SHADOW, core, w_shadow, ([back], second), other, kept)
    (moved,) = on_second_core(SHADOW, core, more[:, BW:], (back, second), "shadow")
    diags = [more[:, :BW], diag1]
    xs = (joined, kept)
    w0, w1, *rest = whiten(reduced(partial), diags)
    w_shadow = behind(w0, 0)
    (given,) = on_second_core(PLAIN, core, w0, xs, "given")
    other = beside(given)
    kept, diag1, more = kept_second(PLAIN, w1, *rest, *xs)
    more = backward(more)
    joined, partial = combine(PLAIN, core, w_shadow, (pieces, moved), other, kept)
    diags = [more[:, :BW], diag1]
    xs = (joined, kept)
    send, w = last(core, thr, reduced(partial), diags, xs)
    got = swap_cores(send)
    packed = last_kept(core, w, xs, got)
    landed = lax.all_to_all(packed, ("zx", "pairs"), split_axis=0, concat_axis=0, tiled=True)
    landed = landed.reshape(8, 8, 4, RB)
    landed = jnp.roll(landed, 1, axis=1).transpose(2, 1, 0, 3)
    return landed.reshape(32, 8 * RB)


def solution(mesh):
    finer = Mesh(mesh.devices.reshape(8, 2, 8), AXES)
    placed = P(("zx", "core"), "pairs")
    return jax.shard_map(
        on_device,
        mesh=finer,
        in_specs=(placed, placed, placed, P("pairs")),
        out_specs=P(AXES, None),
        check_vma=False,
    )
```

```python
import functools

import jax
import jax.numpy as jnp
from jax import lax
from jax.experimental import pallas as pl
from jax.experimental.pallas import tpu as pltpu
from jax.sharding import Mesh, PartitionSpec as P

BW = 128
PW = 2 * BW
RH = 1536
RB = 2 * RH
CH = 512
AXES = ("zx", "core", "pairs")
F32 = jnp.float32
BF16 = jnp.bfloat16
VMEM = pl.BlockSpec(memory_space=pltpu.VMEM)
ANY = pl.BlockSpec(memory_space=pl.ANY)
SMEM = pl.BlockSpec(memory_space=pltpu.SMEM)
NN = (((1,), (0,)), ((), ()))
NT = (((1,), (1,)), ((), ()))


def params(mib=44):
    return pltpu.CompilerParams(vmem_limit_bytes=mib * 1024 * 1024)


def cost(flops, moved):
    return pl.CostEstimate(flops=flops * 30, bytes_accessed=moved, transcendentals=0)


def split(x):
    high = x.astype(BF16)
    return high, (x - high.astype(F32)).astype(BF16)


def mxu(a, b, dims=NN):
    return lax.dot_general(a, b, dims, preferred_element_type=F32)


def dot3(a, b):
    (ah, al), (bh, bl) = a, b
    return mxu(ah, bh) + (mxu(ah, bl) + mxu(al, bh))


def fill_kernel(core_ref, obs_ref, est_ref, mask_ref, keep_ref, send_ref):
    filled = jnp.where(mask_ref[...] == 1, obs_ref[...], est_ref[...])
    first = core_ref[0] == 0
    a = filled[:, :PW]
    b = filled[:, PW:]
    keep_ref[...] = jnp.where(first, a, b).T
    send_ref[...] = jnp.where(first, b, a).T


def fill(core, observed, estimate, mask):
    step = 512
    rows = pl.BlockSpec((step, 2 * PW), lambda i: (i, 0))
    out = pl.BlockSpec((PW, step), lambda i: (0, i))
    return pl.pallas_call(
        fill_kernel,
        grid=(RH // step,),
        in_specs=[SMEM, rows, rows, rows],
        out_specs=[out, out],
        out_shape=[jax.ShapeDtypeStruct((PW, RH), F32)] * 2,
        compiler_params=params(50),
        cost_estimate=cost(10**6, 15 * 10**6),
        name="fill",
    )(core, observed, estimate, mask)


def gram_parts(x_ref):
    hh = jnp.zeros((PW, PW), F32)
    hl = jnp.zeros((PW, PW), F32)
    for j in range(0, RH, CH):
        h, l = split(x_ref[:, j : j + CH])
        hh += mxu(h, h, NT)
        hl += mxu(h, l, NT)
    return hh, hl


def gram_first_kernel(x_ref, hh_ref, hl_ref):
    hh_ref[...], hl_ref[...] = gram_parts(x_ref)


def gram_second_kernel(x_ref, hh_ref, hl_ref, out_ref):
    hh, hl = gram_parts(x_ref)
    hl += hl_ref[...]
    g = hh + hh_ref[...] + (hl + hl.T)
    at_row = lax.broadcasted_iota(jnp.int32, (BW, BW), 0)
    at_col = lax.broadcasted_iota(jnp.int32, (BW, BW), 1)
    d0, d1 = g[:BW, :BW], g[BW:, BW:]
    out_ref[0:BW] = g[:BW, BW:]
    out_ref[BW : 2 * BW] = jnp.where(at_col > at_row, d0, d1)
    on_diag = jnp.sum(jnp.where(at_col == at_row, d0, 0.0), axis=0, keepdims=True)
    out_ref[2 * BW :] = jnp.broadcast_to(on_diag, (8, BW))


def gram_cross_kernel(k_ref, m_ref, *refs):
    out_ref = refs[-1]
    total = jnp.zeros((PW, PW), F32)
    for half in range(2):
        for j in range(0, RH, CH):
            ka = half * RH + j
            ma = (1 - half) * RH + j
            k = jnp.concatenate(split(k_ref[:, ka : ka + CH]), axis=0)
            m = jnp.concatenate(split(m_ref[:, ma : ma + CH]), axis=0)
            total += mxu(k, m, NT)
    out_ref[...] = (total[:BW, :BW] + total[BW:, BW:]) + (total[:BW, BW:] + total[BW:, :BW])


def gram_first(x):
    return pl.pallas_call(
        gram_first_kernel,
        in_specs=[VMEM],
        out_specs=[VMEM] * 2,
        out_shape=[jax.ShapeDtypeStruct((PW, PW), F32)] * 2,
        compiler_params=params(),
        cost_estimate=cost(4 * RH * PW * PW, 3 * 10**6),
        name="gram_first",
    )(x)


def gram_second(x, hh, hl):
    return pl.pallas_call(
        gram_second_kernel,
        in_specs=[VMEM] * 3,
        out_specs=VMEM,
        out_shape=jax.ShapeDtypeStruct((2 * BW + 8, BW), F32),
        compiler_params=params(),
        cost_estimate=cost(4 * RH * PW * PW, 3 * 10**6),
        name="gram_second",
    )(x, hh, hl)


def gram_cross(k, m, *arrived):
    return pl.pallas_call(
        gram_cross_kernel,
        in_specs=[VMEM] * 2 + [ANY] * len(arrived),
        out_specs=VMEM,
        out_shape=jax.ShapeDtypeStruct((BW, BW), F32),
        compiler_params=params(),
        cost_estimate=cost(4 * RH * PW * PW, 3 * 10**6),
        name="gram_cross",
    )(k, m, *arrived)


def newton(gram):
    at_row = lax.broadcasted_iota(jnp.int32, (PW, PW), 0)
    at_col = lax.broadcasted_iota(jnp.int32, (PW, PW), 1)
    on = at_row == at_col
    diag = jnp.where(on, gram, 0.0)
    d_col = jnp.sum(diag, axis=1, keepdims=True) + 1e-06
    d_row = jnp.sum(diag, axis=0, keepdims=True) + 1e-06
    inv_col = 1.0 / jnp.sqrt(d_col)
    inv_row = 1.0 / jnp.sqrt(d_row)
    normed = gram * inv_col * inv_row
    fro = jnp.sqrt(jnp.sum(jnp.sum(normed * normed, axis=1, keepdims=True), axis=0, keepdims=True))
    y = normed / fro
    three = jnp.where(on, 1.5, 0.0)
    t = three - 0.5 * y
    ts = split(t)
    y = dot3(split(y), ts)
    z, zs = t, ts
    ys = split(y)
    t = three - 0.5 * dot3(zs, ys)
    ts = split(t)
    y = dot3(ys, ts)
    z = dot3(ts, zs)
    ys, zs = split(y), split(z)
    t = three - 0.5 * dot3(zs, ys)
    ts = split(t)
    z = dot3(ts, zs)
    return z, y, t, d_col, d_row, inv_row, fro


def gram_of(g_refs, diag_refs):
    total = (g_refs[0][...] + g_refs[1][...]) + (g_refs[2][...] + g_refs[3][...])
    if diag_refs:
        d0, cross, d1 = diag_refs[0][...], total, diag_refs[1][...]
    else:
        cross, both, on_diag = total[:BW], total[BW : 2 * BW], total[2 * BW : 2 * BW + 1]
        at_row = lax.broadcasted_iota(jnp.int32, (BW, BW), 0)
        at_col = lax.broadcasted_iota(jnp.int32, (BW, BW), 1)
        turned = both.T
        d0 = jnp.where(at_col == at_row, on_diag, jnp.where(at_col > at_row, both, turned))
        d1 = jnp.where(at_col > at_row, turned, both)
    top = jnp.concatenate([d0, cross], axis=1)
    bottom = jnp.concatenate([cross.T, d1], axis=1)
    return jnp.concatenate([top, bottom], axis=0)


HALVES = "halves"
CROSSED = (False, True)
SHADOW = (True, False)
PLAIN = (False, False)


PIECES = (RB,)


def rows_of(x_ref, at):
    if isinstance(x_ref, list):
        for piece in x_ref:
            if at < piece.shape[1]:
                return piece[:, at : at + CH]
            at -= piece.shape[1]
    return x_ref[:, at : at + CH]


def columns(x_refs, form, half, j):
    if form == HALVES:
        return x_refs[half][:, j : j + CH]
    ats = [((1 - half) if crossed else half) * RH + j for crossed in form]
    return jnp.concatenate([rows_of(x_ref, at) for x_ref, at in zip(x_refs, ats)], axis=0)


def apply_to(w, x_refs, form, out_ref, offset=None):
    wh, wl = split(w)
    both = jnp.concatenate([wh, wl], axis=0)
    for half in range(2):
        for j in range(0, RH, CH):
            xh, xl = split(columns(x_refs, form, half, j))
            wide = mxu(both, xh)
            value = wide[:BW] + (wide[BW:] + mxu(wh, xl))
            if offset is None:
                out_ref[:, half * RH + j : half * RH + j + CH] = value
            else:
                at = pl.multiple_of((offset if half == 0 else RH - offset) + j, 128)
                out_ref[:, pl.ds(at, CH)] = value


BLOCK = jax.ShapeDtypeStruct((BW, RB), F32)
ROWS_OF_W = jax.ShapeDtypeStruct((BW, PW), F32)
SQUARE = jax.ShapeDtypeStruct((PW, PW), F32)
SCALES = jax.ShapeDtypeStruct((PW, BW), F32)
DIAGONAL = jax.ShapeDtypeStruct((BW, BW), F32)


def call(kernel, ins, outs, name, args):
    return pl.pallas_call(
        kernel,
        in_specs=ins,
        out_specs=[VMEM] * len(outs),
        out_shape=outs,
        compiler_params=params(),
        cost_estimate=cost(10**9, 6 * 10**6),
        name=name,
    )(*args)


def whiten_kernel(first_round, *refs):
    n = 4 if first_round else 6
    g_refs, diag_refs = refs[:4], refs[4:n]
    first_ref, second_ref, z_ref, y_ref, t_ref, d_ref = refs[-6:]
    z, y, t, d_col, d_row, inv_row, fro = newton(gram_of(g_refs, diag_refs))
    wt = jnp.sqrt(d_col) * z.T * (inv_row / jnp.sqrt(fro))
    if first_round:
        apply_to(wt[BW:], refs[n : n + 2], HALVES, second_ref)
        apply_to(wt[:BW], refs[n : n + 2], HALVES, first_ref)
    else:
        first_ref[...] = wt[:BW]
        second_ref[...] = wt[BW:]
    z_ref[...] = z
    y_ref[...] = y
    t_ref[...] = t
    root = jnp.sqrt(d_col) * jnp.sqrt(d_row)
    d_ref[...] = jnp.concatenate([root[:BW, :BW], root[BW:, BW:]], axis=0)


def whiten(grams, diags, xs=(), arrived=()):
    args = [*grams, *diags, *xs, *arrived]
    ins = [VMEM] * (len(args) - len(arrived)) + [ANY] * len(arrived)
    outs = [BLOCK if xs else ROWS_OF_W] * 2 + [SQUARE, SQUARE, SQUARE, SCALES]
    return call(functools.partial(whiten_kernel, bool(xs)), ins, outs, "whiten", args)


def next_diagonals(z_ref, y_ref, t_ref, d_ref):
    ys = split(dot3(split(y_ref[...]), split(t_ref[...])))
    new = dot3(ys, split(z_ref[...]))
    return new[:BW, :BW] * d_ref[:BW], new[BW:, BW:] * d_ref[BW:]


def diagonals_kernel(z_ref, y_ref, t_ref, d_ref, diag0_ref, diag1_ref):
    diag0_ref[...], diag1_ref[...] = next_diagonals(z_ref, y_ref, t_ref, d_ref)


def diagonals(*args):
    return call(diagonals_kernel, [VMEM] * 4, [DIAGONAL, DIAGONAL], "diagonals", args)


def kept_second_kernel(form, w_ref, z_ref, y_ref, t_ref, d_ref, x0_ref, x1_ref, kept_ref, diag_ref, more_ref):
    apply_to(w_ref[...], (x0_ref, x1_ref), form, kept_ref)
    more_ref[:, :BW], diag_ref[...] = next_diagonals(z_ref, y_ref, t_ref, d_ref)
    more_ref[:, BW:] = w_ref[...]


def kept_second(form, *args):
    more = jax.ShapeDtypeStruct((BW, BW + PW), F32)
    kernel = functools.partial(kept_second_kernel, form)
    return call(kernel, [VMEM] * 7, [BLOCK, DIAGONAL, more], "kept_second", args)


def on_second_core_kernel(form, core_ref, w_ref, x0_ref, x1_ref, out_ref, *piece_refs):
    @pl.when(core_ref[0] != 0)
    def _():
        apply_to(w_ref[...], (x0_ref, x1_ref), form, out_ref)
        at = 0
        for piece_ref in piece_refs:
            piece_ref[...] = out_ref[:, at : at + piece_ref.shape[1]]
            at += piece_ref.shape[1]


def on_second_core(form, core, w, xs, name, pieces=()):
    kernel = functools.partial(on_second_core_kernel, form)
    outs = [BLOCK] + [jax.ShapeDtypeStruct((BW, piece), F32) for piece in pieces]
    return call(kernel, [SMEM] + [VMEM] * 3, outs, name, [core, w, *xs])


def combine_kernel(form, n, core_ref, w_ref, *refs):
    s0_ref = list(refs[:n])
    s1_ref, other_ref, kept_ref = refs[n : n + 3]
    in_ref, out_ref = refs[-2:]

    @pl.when(core_ref[0] == 0)
    def _():
        in_ref[:, :RH] = other_ref[:, RH:]
        in_ref[:, RH:] = other_ref[:, :RH]

    @pl.when(core_ref[0] != 0)
    def _():
        apply_to(w_ref[...], (s0_ref, s1_ref), form, in_ref)

    total = jnp.zeros((PW, PW), F32)
    for j in range(0, RB, CH):
        a = jnp.concatenate(split(in_ref[:, j : j + CH]), axis=0)
        b = jnp.concatenate(split(kept_ref[:, j : j + CH]), axis=0)
        total += mxu(a, b, NT)
    out_ref[...] = (total[:BW, :BW] + total[BW:, BW:]) + (total[:BW, BW:] + total[BW:, :BW])


def combine(form, core, w, shadow, other, kept, *arrived):
    pieces, second = shadow
    kernel = functools.partial(combine_kernel, form, len(pieces))
    args = [core, w, *pieces, second, other, kept, *arrived]
    ins = [SMEM] + [VMEM] * (len(pieces) + 4) + [ANY] * len(arrived)
    return call(kernel, ins, [BLOCK, DIAGONAL], "combine", args)


def by_core(w, even):
    parts = [w[i : i + 32] for i in range(0, PW, 32)]
    evens = jnp.concatenate(parts[0::2], axis=0)
    odds = jnp.concatenate(parts[1::2], axis=0)
    return jnp.where(even, evens, odds)


def last_kernel(core_ref, thr_ref, *refs):
    g_refs, diag_refs, x_refs = refs[:4], refs[4:6], refs[6:8]
    send_ref, w_ref = refs[8:]
    core = core_ref[0]
    z, y, t, d_col, d_row, inv_row, fro = newton(gram_of(g_refs, diag_refs))
    y = dot3(split(y), split(t))
    norm = jnp.sqrt(d_col * jnp.sum(z * y, axis=1, keepdims=True) + 1e-06)
    at_row = lax.broadcasted_iota(jnp.int32, (PW, PW), 0)
    at_col = lax.broadcasted_iota(jnp.int32, (PW, PW), 1)
    thr_row = jnp.where(core == 0, thr_ref[:, :PW], thr_ref[:, PW:])
    thr = jnp.sum(jnp.where(at_row == at_col, thr_row, 0.0), axis=1, keepdims=True)
    factor = jnp.maximum(norm - thr, 0.0) / norm
    wt = (factor * jnp.sqrt(d_col)) * z.T * (inv_row / jnp.sqrt(fro))
    apply_to(by_core(wt, core != 0), x_refs, PLAIN, send_ref, core * RH)
    w_ref[...] = by_core(wt, core == 0)


def last(core, thr, grams, diags, xs):
    return pl.pallas_call(
        last_kernel,
        in_specs=[SMEM] + [VMEM] * 9,
        out_specs=[VMEM] * 2,
        out_shape=[jax.ShapeDtypeStruct((BW, RB), F32), jax.ShapeDtypeStruct((BW, PW), F32)],
        compiler_params=params(),
        cost_estimate=cost(10**9, 6 * 10**6),
        name="last",
    )(core, thr, *grams, *diags, *xs)


def last_kept_kernel(core_ref, w_ref, k_ref, m_ref, got_ref, out_ref):
    core = core_ref[0]
    wh, wl = split(w_ref[...])
    both = jnp.concatenate([wh, wl], axis=0)
    mine, other = core * 32, 32 - core * 32
    for half in range(2):
        for j in range(0, RH, CH):
            xh, xl = split(columns((k_ref, m_ref), PLAIN, half, j))
            wide = mxu(both, xh)
            value = wide[:BW] + (wide[BW:] + mxu(wh, xl))
            at = pl.multiple_of((core * RH if half == 0 else RH - core * RH) + j, 128)
            for d in range(32):
                out_ref[mine + d, :, pl.ds(at, CH)] = value[4 * d : 4 * d + 4]
    for j in range(0, RB, CH):
        for d in range(32):
            out_ref[other + d, :, j : j + CH] = got_ref[4 * d : 4 * d + 4, j : j + CH]


def last_kept(core, w, xs, got):
    return pl.pallas_call(
        last_kept_kernel,
        in_specs=[SMEM] + [VMEM] * 4,
        out_specs=VMEM,
        out_shape=jax.ShapeDtypeStruct((64, 4, RB), F32),
        compiler_params=params(),
        cost_estimate=cost(10**9, 6 * 10**6),
        name="last_kept",
    )(core, w, *xs, got)


def place_kernel(in_ref, out_ref):
    for w in range(4):
        for j in range(0, RB, CH):
            rows = in_ref[:, w, j : j + CH]
            out_ref[8 * w : 8 * w + 8, j : j + CH] = jnp.concatenate([rows[7:], rows[:7]], axis=0)


def place(landed):
    return pl.pallas_call(
        place_kernel,
        grid=(8,),
        in_specs=[pl.BlockSpec((8, 4, RB), lambda i: (i, 0, 0))],
        out_specs=pl.BlockSpec((32, RB), lambda i: (0, i)),
        out_shape=jax.ShapeDtypeStruct((32, 8 * RB), F32),
        compiler_params=params(),
        cost_estimate=cost(10**6, 6 * 10**6),
        name="place",
    )(landed)


def to(block, where):
    route = []
    for i in range(8):
        for c in range(2):
            for g in range(8):
                goal = where(i, c, g)
                if goal is not None:
                    ti, tc, tg = goal
                    route.append(((i * 2 + c) * 8 + g, (ti * 2 + tc) * 8 + tg))
    return lax.ppermute(block, AXES, route)


def swap_cores(block):
    return to(block, lambda i, c, g: (i, 1 - c, g))


def onward(block):
    return to(block, lambda i, c, g: (i, 1, g) if c == 0 else (i, 0, (g + 1) % 8))


def backward(block):
    return to(block, lambda i, c, g: (i, 1, (g - 1) % 8) if c == 0 else (i, 0, g))


def behind(block, core):
    return to(block, lambda i, c, g: (i, 1, (g - 1) % 8) if c == core else None)


def beside(block):
    return to(block, lambda i, c, g: (i, 0, g) if c == 1 else None)


def reduced(partial):
    pair = partial + to(partial, lambda i, c, g: (i ^ 1, c, g))
    return [pair] + [to(pair, lambda i, c, g, k=k: (i ^ k, c, g)) for k in (2, 4, 6)]


def on_device(observed, estimate, mask, threshold):
    core = lax.axis_index("core").reshape(1).astype(jnp.int32)
    thr = to(threshold.reshape(1, -1), lambda i, c, g: (i, c, (g - 1) % 8))
    keep, send = fill(core, observed, estimate, mask)
    got = swap_cores(send)
    grams = reduced(gram_second(got, *gram_first(keep)))
    first, second, *rest = whiten(grams, [], (keep, got))
    joined = onward(second)
    back = behind(first, 0)
    diag0, diag1 = diagonals(*rest)
    diags = [diag0, onward(diag1)]
    partial = gram_cross(first, joined, back, thr)
    xs = (first, joined)
    w0, w1, *rest = whiten(reduced(partial), diags)
    w_shadow = behind(w0, 0)
    (given,) = on_second_core(CROSSED, core, w0, xs, "given")
    other = beside(given)
    pieces = [behind(given, 1)]
    kept, diag1, more = kept_second(CROSSED, w1, *rest, *xs)
    more = backward(more)
    joined, partial = combine(SHADOW, core, w_shadow, ([back], second), other, kept)
    (moved,) = on_second_core(SHADOW, core, more[:, BW:], (back, second), "shadow")
    diags = [more[:, :BW], diag1]
    xs = (joined, kept)
    w0, w1, *rest = whiten(reduced(partial), diags)
    w_shadow = behind(w0, 0)
    (given,) = on_second_core(PLAIN, core, w0, xs, "given")
    other = beside(given)
    kept, diag1, more = kept_second(PLAIN, w1, *rest, *xs)
    more = backward(more)
    joined, partial = combine(PLAIN, core, w_shadow, (pieces, moved), other, kept)
    diags = [more[:, :BW], diag1]
    xs = (joined, kept)
    send, w = last(core, thr, reduced(partial), diags, xs)
    got = swap_cores(send)
    packed = last_kept(core, w, xs, got)
    landed = lax.all_to_all(packed, ("zx", "pairs"), split_axis=0, concat_axis=0, tiled=True)
    return place(landed)


def solution(mesh):
    finer = Mesh(mesh.devices.reshape(8, 2, 8), AXES)
    placed = P(("zx", "core"), "pairs")
    return jax.shard_map(
        on_device,
        mesh=finer,
        in_specs=(placed, placed, placed, P("pairs")),
        out_specs=P(AXES, None),
        check_vma=False,
    )
```

```python
import functools

import jax
import jax.numpy as jnp
from jax import lax
from jax.experimental import pallas as pl
from jax.experimental.pallas import tpu as pltpu
from jax.sharding import Mesh, PartitionSpec as P

BW = 128
PW = 2 * BW
RH = 1536
RB = 2 * RH
CH = 512
AXES = ("zx", "core", "pairs")
F32 = jnp.float32
BF16 = jnp.bfloat16
VMEM = pl.BlockSpec(memory_space=pltpu.VMEM)
ANY = pl.BlockSpec(memory_space=pl.ANY)
SMEM = pl.BlockSpec(memory_space=pltpu.SMEM)
NN = (((1,), (0,)), ((), ()))
NT = (((1,), (1,)), ((), ()))


def params(mib=44):
    return pltpu.CompilerParams(vmem_limit_bytes=mib * 1024 * 1024)


def cost(flops, moved):
    return pl.CostEstimate(flops=flops * 30, bytes_accessed=moved, transcendentals=0)


def split(x):
    high = x.astype(BF16)
    return high, (x - high.astype(F32)).astype(BF16)


def mxu(a, b, dims=NN):
    return lax.dot_general(a, b, dims, preferred_element_type=F32)


def dot3(a, b):
    (ah, al), (bh, bl) = a, b
    return mxu(ah, bh) + (mxu(ah, bl) + mxu(al, bh))


def fill_kernel(core_ref, obs_ref, est_ref, mask_ref, keep_ref, send_ref):
    filled = jnp.where(mask_ref[...] == 1, obs_ref[...], est_ref[...])
    first = core_ref[0] == 0
    a = filled[:, :PW]
    b = filled[:, PW:]
    keep_ref[...] = jnp.where(first, a, b).T
    send_ref[...] = jnp.where(first, b, a).T


def fill(core, observed, estimate, mask):
    step = 512
    rows = pl.BlockSpec((step, 2 * PW), lambda i: (i, 0))
    out = pl.BlockSpec((PW, step), lambda i: (0, i))
    return pl.pallas_call(
        fill_kernel,
        grid=(RH // step,),
        in_specs=[SMEM, rows, rows, rows],
        out_specs=[out, out],
        out_shape=[jax.ShapeDtypeStruct((PW, RH), F32)] * 2,
        compiler_params=params(50),
        cost_estimate=cost(10**6, 15 * 10**6),
        name="fill",
    )(core, observed, estimate, mask)


def gram_parts(x_ref):
    hh = jnp.zeros((PW, PW), F32)
    hl = jnp.zeros((PW, PW), F32)
    for j in range(0, RH, CH):
        h, l = split(x_ref[:, j : j + CH])
        hh += mxu(h, h, NT)
        hl += mxu(h, l, NT)
    return hh, hl


def gram_first_kernel(x_ref, hh_ref, hl_ref):
    hh_ref[...], hl_ref[...] = gram_parts(x_ref)


def gram_second_kernel(x_ref, hh_ref, hl_ref, out_ref):
    hh, hl = gram_parts(x_ref)
    hl += hl_ref[...]
    g = hh + hh_ref[...] + (hl + hl.T)
    at_row = lax.broadcasted_iota(jnp.int32, (BW, BW), 0)
    at_col = lax.broadcasted_iota(jnp.int32, (BW, BW), 1)
    d0, d1 = g[:BW, :BW], g[BW:, BW:]
    out_ref[0:BW] = g[:BW, BW:]
    out_ref[BW : 2 * BW] = jnp.where(at_col > at_row, d0, d1)
    on_diag = jnp.sum(jnp.where(at_col == at_row, d0, 0.0), axis=0, keepdims=True)
    out_ref[2 * BW :] = jnp.broadcast_to(on_diag, (8, BW))


def gram_cross_kernel(k_ref, m_ref, *refs):
    out_ref = refs[-1]
    total = jnp.zeros((PW, PW), F32)
    for half in range(2):
        for j in range(0, RH, CH):
            ka = half * RH + j
            ma = (1 - half) * RH + j
            k = jnp.concatenate(split(k_ref[:, ka : ka + CH]), axis=0)
            m = jnp.concatenate(split(m_ref[:, ma : ma + CH]), axis=0)
            total += mxu(k, m, NT)
    out_ref[...] = (total[:BW, :BW] + total[BW:, BW:]) + (total[:BW, BW:] + total[BW:, :BW])


def gram_first(x):
    return pl.pallas_call(
        gram_first_kernel,
        in_specs=[VMEM],
        out_specs=[VMEM] * 2,
        out_shape=[jax.ShapeDtypeStruct((PW, PW), F32)] * 2,
        compiler_params=params(),
        cost_estimate=cost(4 * RH * PW * PW, 3 * 10**6),
        name="gram_first",
    )(x)


def gram_second(x, hh, hl):
    return pl.pallas_call(
        gram_second_kernel,
        in_specs=[VMEM] * 3,
        out_specs=VMEM,
        out_shape=jax.ShapeDtypeStruct((2 * BW + 8, BW), F32),
        compiler_params=params(),
        cost_estimate=cost(4 * RH * PW * PW, 3 * 10**6),
        name="gram_second",
    )(x, hh, hl)


def gram_cross(k, m, *arrived):
    return pl.pallas_call(
        gram_cross_kernel,
        in_specs=[VMEM] * 2 + [ANY] * len(arrived),
        out_specs=VMEM,
        out_shape=jax.ShapeDtypeStruct((BW, BW), F32),
        compiler_params=params(),
        cost_estimate=cost(4 * RH * PW * PW, 3 * 10**6),
        name="gram_cross",
    )(k, m, *arrived)


def newton(gram):
    at_row = lax.broadcasted_iota(jnp.int32, (PW, PW), 0)
    at_col = lax.broadcasted_iota(jnp.int32, (PW, PW), 1)
    on = at_row == at_col
    diag = jnp.where(on, gram, 0.0)
    d_col = jnp.sum(diag, axis=1, keepdims=True) + 1e-06
    d_row = jnp.sum(diag, axis=0, keepdims=True) + 1e-06
    inv_col = 1.0 / jnp.sqrt(d_col)
    inv_row = 1.0 / jnp.sqrt(d_row)
    normed = gram * inv_col * inv_row
    fro = jnp.sqrt(jnp.sum(jnp.sum(normed * normed, axis=1, keepdims=True), axis=0, keepdims=True))
    y = normed / fro
    three = jnp.where(on, 1.5, 0.0)
    t = three - 0.5 * y
    ts = split(t)
    y = dot3(split(y), ts)
    z, zs = t, ts
    ys = split(y)
    t = three - 0.5 * dot3(zs, ys)
    ts = split(t)
    y = dot3(ys, ts)
    z = dot3(ts, zs)
    ys, zs = split(y), split(z)
    t = three - 0.5 * dot3(zs, ys)
    ts = split(t)
    z = dot3(ts, zs)
    return z, y, t, d_col, d_row, inv_row, fro


def gram_of(g_refs, diag_refs):
    total = (g_refs[0][...] + g_refs[1][...]) + (g_refs[2][...] + g_refs[3][...])
    if diag_refs:
        d0, cross, d1 = diag_refs[0][...], total, diag_refs[1][...]
    else:
        cross, both, on_diag = total[:BW], total[BW : 2 * BW], total[2 * BW : 2 * BW + 1]
        at_row = lax.broadcasted_iota(jnp.int32, (BW, BW), 0)
        at_col = lax.broadcasted_iota(jnp.int32, (BW, BW), 1)
        turned = both.T
        d0 = jnp.where(at_col == at_row, on_diag, jnp.where(at_col > at_row, both, turned))
        d1 = jnp.where(at_col > at_row, turned, both)
    top = jnp.concatenate([d0, cross], axis=1)
    bottom = jnp.concatenate([cross.T, d1], axis=1)
    return jnp.concatenate([top, bottom], axis=0)


HALVES = "halves"
CROSSED = (False, True)
SHADOW = (True, False)
PLAIN = (False, False)


PIECES = (RB,)


def rows_of(x_ref, at):
    if isinstance(x_ref, list):
        for piece in x_ref:
            if at < piece.shape[1]:
                return piece[:, at : at + CH]
            at -= piece.shape[1]
    return x_ref[:, at : at + CH]


def columns(x_refs, form, half, j):
    if form == HALVES:
        return x_refs[half][:, j : j + CH]
    ats = [((1 - half) if crossed else half) * RH + j for crossed in form]
    return jnp.concatenate([rows_of(x_ref, at) for x_ref, at in zip(x_refs, ats)], axis=0)


def apply_to(w, x_refs, form, out_ref, offset=None):
    wh, wl = split(w)
    both = jnp.concatenate([wh, wl], axis=0)
    for half in range(2):
        for j in range(0, RH, CH):
            xh, xl = split(columns(x_refs, form, half, j))
            wide = mxu(both, xh)
            value = wide[:BW] + (wide[BW:] + mxu(wh, xl))
            if offset is None:
                out_ref[:, half * RH + j : half * RH + j + CH] = value
            else:
                at = pl.multiple_of((offset if half == 0 else RH - offset) + j, 128)
                out_ref[:, pl.ds(at, CH)] = value


BLOCK = jax.ShapeDtypeStruct((BW, RB), F32)
ROWS_OF_W = jax.ShapeDtypeStruct((BW, PW), F32)
SQUARE = jax.ShapeDtypeStruct((PW, PW), F32)
SCALES = jax.ShapeDtypeStruct((PW, BW), F32)
DIAGONAL = jax.ShapeDtypeStruct((BW, BW), F32)


def call(kernel, ins, outs, name, args):
    return pl.pallas_call(
        kernel,
        in_specs=ins,
        out_specs=[VMEM] * len(outs),
        out_shape=outs,
        compiler_params=params(),
        cost_estimate=cost(10**9, 6 * 10**6),
        name=name,
    )(*args)


def whiten_kernel(first_round, *refs):
    n = 4 if first_round else 6
    g_refs, diag_refs = refs[:4], refs[4:n]
    first_ref, second_ref, z_ref, y_ref, t_ref, d_ref = refs[-6:]
    z, y, t, d_col, d_row, inv_row, fro = newton(gram_of(g_refs, diag_refs))
    wt = jnp.sqrt(d_col) * z.T * (inv_row / jnp.sqrt(fro))
    if first_round:
        apply_to(wt[BW:], refs[n : n + 2], HALVES, second_ref)
        apply_to(wt[:BW], refs[n : n + 2], HALVES, first_ref)
    else:
        first_ref[...] = wt[:BW]
        second_ref[...] = wt[BW:]
    z_ref[...] = z
    y_ref[...] = y
    t_ref[...] = t
    root = jnp.sqrt(d_col) * jnp.sqrt(d_row)
    d_ref[...] = jnp.concatenate([root[:BW, :BW], root[BW:, BW:]], axis=0)


def whiten(grams, diags, xs=(), arrived=()):
    args = [*grams, *diags, *xs, *arrived]
    ins = [VMEM] * (len(args) - len(arrived)) + [ANY] * len(arrived)
    outs = [BLOCK if xs else ROWS_OF_W] * 2 + [SQUARE, SQUARE, SQUARE, SCALES]
    return call(functools.partial(whiten_kernel, bool(xs)), ins, outs, "whiten", args)


def next_diagonals(z_ref, y_ref, t_ref, d_ref):
    ys = split(dot3(split(y_ref[...]), split(t_ref[...])))
    new = dot3(ys, split(z_ref[...]))
    return new[:BW, :BW] * d_ref[:BW], new[BW:, BW:] * d_ref[BW:]


def diagonals_kernel(z_ref, y_ref, t_ref, d_ref, diag0_ref, diag1_ref):
    diag0_ref[...], diag1_ref[...] = next_diagonals(z_ref, y_ref, t_ref, d_ref)


def diagonals(*args):
    return call(diagonals_kernel, [VMEM] * 4, [DIAGONAL, DIAGONAL], "diagonals", args)


def kept_second_kernel(form, w_ref, z_ref, y_ref, t_ref, d_ref, x0_ref, x1_ref, kept_ref, diag_ref, more_ref):
    apply_to(w_ref[...], (x0_ref, x1_ref), form, kept_ref)
    more_ref[:, :BW], diag_ref[...] = next_diagonals(z_ref, y_ref, t_ref, d_ref)
    more_ref[:, BW:] = w_ref[...]


def kept_second(form, *args):
    more = jax.ShapeDtypeStruct((BW, BW + PW), F32)
    kernel = functools.partial(kept_second_kernel, form)
    return call(kernel, [VMEM] * 7, [BLOCK, DIAGONAL, more], "kept_second", args)


def on_second_core_kernel(form, core_ref, w_ref, x0_ref, x1_ref, out_ref, *piece_refs):
    @pl.when(core_ref[0] != 0)
    def _():
        apply_to(w_ref[...], (x0_ref, x1_ref), form, out_ref)
        at = 0
        for piece_ref in piece_refs:
            piece_ref[...] = out_ref[:, at : at + piece_ref.shape[1]]
            at += piece_ref.shape[1]


def on_second_core(form, core, w, xs, name, pieces=()):
    kernel = functools.partial(on_second_core_kernel, form)
    outs = [BLOCK] + [jax.ShapeDtypeStruct((BW, piece), F32) for piece in pieces]
    return call(kernel, [SMEM] + [VMEM] * 3, outs, name, [core, w, *xs])


def combine_kernel(form, n, core_ref, w_ref, *refs):
    s0_ref = list(refs[:n])
    s1_ref, other_ref, kept_ref = refs[n : n + 3]
    in_ref, out_ref = refs[-2:]

    @pl.when(core_ref[0] == 0)
    def _():
        in_ref[:, :RH] = other_ref[:, RH:]
        in_ref[:, RH:] = other_ref[:, :RH]

    @pl.when(core_ref[0] != 0)
    def _():
        apply_to(w_ref[...], (s0_ref, s1_ref), form, in_ref)

    total = jnp.zeros((PW, PW), F32)
    for j in range(0, RB, CH):
        a = jnp.concatenate(split(in_ref[:, j : j + CH]), axis=0)
        b = jnp.concatenate(split(kept_ref[:, j : j + CH]), axis=0)
        total += mxu(a, b, NT)
    out_ref[...] = (total[:BW, :BW] + total[BW:, BW:]) + (total[:BW, BW:] + total[BW:, :BW])


def combine(form, core, w, shadow, other, kept, *arrived):
    pieces, second = shadow
    kernel = functools.partial(combine_kernel, form, len(pieces))
    args = [core, w, *pieces, second, other, kept, *arrived]
    ins = [SMEM] + [VMEM] * (len(pieces) + 4) + [ANY] * len(arrived)
    return call(kernel, ins, [BLOCK, DIAGONAL], "combine", args)


def by_core(w, even):
    parts = [w[i : i + 32] for i in range(0, PW, 32)]
    evens = jnp.concatenate(parts[0::2], axis=0)
    odds = jnp.concatenate(parts[1::2], axis=0)
    return jnp.where(even, evens, odds)


def last_kernel(core_ref, thr_ref, *refs):
    g_refs, diag_refs, x_refs = refs[:4], refs[4:6], refs[6:8]
    send_ref, w_ref = refs[8:]
    core = core_ref[0]
    z, y, t, d_col, d_row, inv_row, fro = newton(gram_of(g_refs, diag_refs))
    y = dot3(split(y), split(t))
    norm = jnp.sqrt(d_col * jnp.sum(z * y, axis=1, keepdims=True) + 1e-06)
    at_row = lax.broadcasted_iota(jnp.int32, (PW, PW), 0)
    at_col = lax.broadcasted_iota(jnp.int32, (PW, PW), 1)
    thr_row = jnp.where(core == 0, thr_ref[:, :PW], thr_ref[:, PW:])
    thr = jnp.sum(jnp.where(at_row == at_col, thr_row, 0.0), axis=1, keepdims=True)
    factor = jnp.maximum(norm - thr, 0.0) / norm
    wt = (factor * jnp.sqrt(d_col)) * z.T * (inv_row / jnp.sqrt(fro))
    apply_to(by_core(wt, core != 0), x_refs, PLAIN, send_ref, core * RH)
    w_ref[...] = by_core(wt, core == 0)


def last(core, thr, grams, diags, xs):
    return pl.pallas_call(
        last_kernel,
        in_specs=[SMEM] + [VMEM] * 9,
        out_specs=[VMEM] * 2,
        out_shape=[jax.ShapeDtypeStruct((BW, RB), F32), jax.ShapeDtypeStruct((BW, PW), F32)],
        compiler_params=params(),
        cost_estimate=cost(10**9, 6 * 10**6),
        name="last",
    )(core, thr, *grams, *diags, *xs)


def last_kept_kernel(core_ref, w_ref, k_ref, m_ref, got_ref, out_ref):
    core = core_ref[0]
    wh, wl = split(w_ref[...])
    both = jnp.concatenate([wh, wl], axis=0)
    mine, other = core * 4, 4 - core * 4
    for half in range(2):
        for j in range(0, RH, CH):
            xh, xl = split(columns((k_ref, m_ref), PLAIN, half, j))
            wide = mxu(both, xh)
            value = wide[:BW] + (wide[BW:] + mxu(wh, xl))
            at = pl.multiple_of((core * RH if half == 0 else RH - core * RH) + j, 128)
            for d in range(32):
                out_ref[d % 8 * 8 + d // 8 + mine, :, pl.ds(at, CH)] = value[4 * d : 4 * d + 4]
    for j in range(0, RB, CH):
        for d in range(32):
            out_ref[d % 8 * 8 + d // 8 + other, :, j : j + CH] = got_ref[4 * d : 4 * d + 4, j : j + CH]


def last_kept(core, w, xs, got):
    return pl.pallas_call(
        last_kept_kernel,
        in_specs=[SMEM] + [VMEM] * 4,
        out_specs=VMEM,
        out_shape=jax.ShapeDtypeStruct((64, 4, RB), F32),
        compiler_params=params(),
        cost_estimate=cost(10**9, 6 * 10**6),
        name="last_kept",
    )(core, w, *xs, got)


def place_kernel(in_ref, out_ref):
    for w in range(4):
        for j in range(0, RB, CH):
            rows = in_ref[:, 0, w, j : j + CH]
            out_ref[8 * w : 8 * w + 8, j : j + CH] = jnp.concatenate([rows[7:], rows[:7]], axis=0)


def place(landed):
    return pl.pallas_call(
        place_kernel,
        grid=(8,),
        in_specs=[pl.BlockSpec((8, 1, 4, RB), lambda i: (0, i, 0, 0))],
        out_specs=pl.BlockSpec((32, RB), lambda i: (0, i)),
        out_shape=jax.ShapeDtypeStruct((32, 8 * RB), F32),
        compiler_params=params(),
        cost_estimate=cost(10**6, 6 * 10**6),
        name="place",
    )(landed)


def to(block, where):
    route = []
    for i in range(8):
        for c in range(2):
            for g in range(8):
                goal = where(i, c, g)
                if goal is not None:
                    ti, tc, tg = goal
                    route.append(((i * 2 + c) * 8 + g, (ti * 2 + tc) * 8 + tg))
    return lax.ppermute(block, AXES, route)


def swap_cores(block):
    return to(block, lambda i, c, g: (i, 1 - c, g))


def onward(block):
    return to(block, lambda i, c, g: (i, 1, g) if c == 0 else (i, 0, (g + 1) % 8))


def backward(block):
    return to(block, lambda i, c, g: (i, 1, (g - 1) % 8) if c == 0 else (i, 0, g))


def behind(block, core):
    return to(block, lambda i, c, g: (i, 1, (g - 1) % 8) if c == core else None)


def beside(block):
    return to(block, lambda i, c, g: (i, 0, g) if c == 1 else None)


def reduced(partial):
    pair = partial + to(partial, lambda i, c, g: (i ^ 1, c, g))
    return [pair] + [to(pair, lambda i, c, g, k=k: (i ^ k, c, g)) for k in (2, 4, 6)]


def on_device(observed, estimate, mask, threshold):
    core = lax.axis_index("core").reshape(1).astype(jnp.int32)
    thr = to(threshold.reshape(1, -1), lambda i, c, g: (i, c, (g - 1) % 8))
    keep, send = fill(core, observed, estimate, mask)
    got = swap_cores(send)
    grams = reduced(gram_second(got, *gram_first(keep)))
    first, second, *rest = whiten(grams, [], (keep, got))
    joined = onward(second)
    back = behind(first, 0)
    diag0, diag1 = diagonals(*rest)
    diags = [diag0, onward(diag1)]
    partial = gram_cross(first, joined, back, thr)
    xs = (first, joined)
    w0, w1, *rest = whiten(reduced(partial), diags)
    w_shadow = behind(w0, 0)
    (given,) = on_second_core(CROSSED, core, w0, xs, "given")
    other = beside(given)
    pieces = [behind(given, 1)]
    kept, diag1, more = kept_second(CROSSED, w1, *rest, *xs)
    more = backward(more)
    joined, partial = combine(SHADOW, core, w_shadow, ([back], second), other, kept)
    (moved,) = on_second_core(SHADOW, core, more[:, BW:], (back, second), "shadow")
    diags = [more[:, :BW], diag1]
    xs = (joined, kept)
    w0, w1, *rest = whiten(reduced(partial), diags)
    w_shadow = behind(w0, 0)
    (given,) = on_second_core(PLAIN, core, w0, xs, "given")
    other = beside(given)
    kept, diag1, more = kept_second(PLAIN, w1, *rest, *xs)
    more = backward(more)
    joined, partial = combine(PLAIN, core, w_shadow, (pieces, moved), other, kept)
    diags = [more[:, :BW], diag1]
    xs = (joined, kept)
    send, w = last(core, thr, reduced(partial), diags, xs)
    got = swap_cores(send)
    packed = last_kept(core, w, xs, got)
    landed = lax.all_to_all(packed, ("pairs", "zx"), split_axis=0, concat_axis=0, tiled=True)
    return place(landed.reshape(8, 8, 4, RB))


def solution(mesh):
    finer = Mesh(mesh.devices.reshape(8, 2, 8), AXES)
    placed = P(("zx", "core"), "pairs")
    return jax.shard_map(
        on_device,
        mesh=finer,
        in_specs=(placed, placed, placed, P("pairs")),
        out_specs=P(AXES, None),
        check_vma=False,
    )
```

```python
import functools

import jax
import jax.numpy as jnp
from jax import lax
from jax.experimental import pallas as pl
from jax.experimental.pallas import tpu as pltpu
from jax.sharding import Mesh, PartitionSpec as P

BW = 128
PW = 2 * BW
RH = 1536
RB = 2 * RH
CH = 768
AXES = ("zx", "core", "pairs")
F32 = jnp.float32
BF16 = jnp.bfloat16
VMEM = pl.BlockSpec(memory_space=pltpu.VMEM)
ANY = pl.BlockSpec(memory_space=pl.ANY)
SMEM = pl.BlockSpec(memory_space=pltpu.SMEM)
NN = (((1,), (0,)), ((), ()))
NT = (((1,), (1,)), ((), ()))


def params(mib=44):
    return pltpu.CompilerParams(vmem_limit_bytes=mib * 1024 * 1024)


def cost(flops, moved):
    return pl.CostEstimate(flops=flops * 30, bytes_accessed=moved, transcendentals=0)


def split(x):
    high = x.astype(BF16)
    return high, (x - high.astype(F32)).astype(BF16)


def mxu(a, b, dims=NN):
    return lax.dot_general(a, b, dims, preferred_element_type=F32)


def dot3(a, b):
    (ah, al), (bh, bl) = a, b
    return mxu(ah, bh) + (mxu(ah, bl) + mxu(al, bh))


def fill_kernel(core_ref, obs_ref, est_ref, mask_ref, keep_ref, send_ref):
    filled = jnp.where(mask_ref[...] == 1, obs_ref[...], est_ref[...])
    first = core_ref[0] == 0
    a = filled[:, :PW]
    b = filled[:, PW:]
    keep_ref[...] = jnp.where(first, a, b).T
    send_ref[...] = jnp.where(first, b, a).T


def fill(core, observed, estimate, mask):
    step = 512
    rows = pl.BlockSpec((step, 2 * PW), lambda i: (i, 0))
    out = pl.BlockSpec((PW, step), lambda i: (0, i))
    return pl.pallas_call(
        fill_kernel,
        grid=(RH // step,),
        in_specs=[SMEM, rows, rows, rows],
        out_specs=[out, out],
        out_shape=[jax.ShapeDtypeStruct((PW, RH), F32)] * 2,
        compiler_params=params(50),
        cost_estimate=cost(10**6, 15 * 10**6),
        name="fill",
    )(core, observed, estimate, mask)


def gram_parts(x_ref):
    hh = jnp.zeros((PW, PW), F32)
    hl = jnp.zeros((PW, PW), F32)
    for j in range(0, RH, CH):
        h, l = split(x_ref[:, j : j + CH])
        hh += mxu(h, h, NT)
        hl += mxu(h, l, NT)
    return hh, hl


def gram_first_kernel(x_ref, hh_ref, hl_ref):
    hh_ref[...], hl_ref[...] = gram_parts(x_ref)


def gram_second_kernel(x_ref, hh_ref, hl_ref, out_ref):
    hh, hl = gram_parts(x_ref)
    hl += hl_ref[...]
    g = hh + hh_ref[...] + (hl + hl.T)
    at_row = lax.broadcasted_iota(jnp.int32, (BW, BW), 0)
    at_col = lax.broadcasted_iota(jnp.int32, (BW, BW), 1)
    d0, d1 = g[:BW, :BW], g[BW:, BW:]
    out_ref[0:BW] = g[:BW, BW:]
    out_ref[BW : 2 * BW] = jnp.where(at_col > at_row, d0, d1)
    on_diag = jnp.sum(jnp.where(at_col == at_row, d0, 0.0), axis=0, keepdims=True)
    out_ref[2 * BW :] = jnp.broadcast_to(on_diag, (8, BW))


def gram_cross_kernel(k_ref, m_ref, *refs):
    out_ref = refs[-1]
    total = jnp.zeros((PW, PW), F32)
    for half in range(2):
        for j in range(0, RH, CH):
            ka = half * RH + j
            ma = (1 - half) * RH + j
            k = jnp.concatenate(split(k_ref[:, ka : ka + CH]), axis=0)
            m = jnp.concatenate(split(m_ref[:, ma : ma + CH]), axis=0)
            total += mxu(k, m, NT)
    out_ref[...] = (total[:BW, :BW] + total[BW:, BW:]) + (total[:BW, BW:] + total[BW:, :BW])


def gram_first(x):
    return pl.pallas_call(
        gram_first_kernel,
        in_specs=[VMEM],
        out_specs=[VMEM] * 2,
        out_shape=[jax.ShapeDtypeStruct((PW, PW), F32)] * 2,
        compiler_params=params(),
        cost_estimate=cost(4 * RH * PW * PW, 3 * 10**6),
        name="gram_first",
    )(x)


def gram_second(x, hh, hl):
    return pl.pallas_call(
        gram_second_kernel,
        in_specs=[VMEM] * 3,
        out_specs=VMEM,
        out_shape=jax.ShapeDtypeStruct((2 * BW + 8, BW), F32),
        compiler_params=params(),
        cost_estimate=cost(4 * RH * PW * PW, 3 * 10**6),
        name="gram_second",
    )(x, hh, hl)


def gram_cross(k, m, *arrived):
    return pl.pallas_call(
        gram_cross_kernel,
        in_specs=[VMEM] * 2 + [ANY] * len(arrived),
        out_specs=VMEM,
        out_shape=jax.ShapeDtypeStruct((BW, BW), F32),
        compiler_params=params(),
        cost_estimate=cost(4 * RH * PW * PW, 3 * 10**6),
        name="gram_cross",
    )(k, m, *arrived)


def newton(gram):
    at_row = lax.broadcasted_iota(jnp.int32, (PW, PW), 0)
    at_col = lax.broadcasted_iota(jnp.int32, (PW, PW), 1)
    on = at_row == at_col
    diag = jnp.where(on, gram, 0.0)
    d_col = jnp.sum(diag, axis=1, keepdims=True) + 1e-06
    d_row = jnp.sum(diag, axis=0, keepdims=True) + 1e-06
    inv_col = 1.0 / jnp.sqrt(d_col)
    inv_row = 1.0 / jnp.sqrt(d_row)
    normed = gram * inv_col * inv_row
    fro = jnp.sqrt(jnp.sum(jnp.sum(normed * normed, axis=1, keepdims=True), axis=0, keepdims=True))
    y = normed / fro
    three = jnp.where(on, 1.5, 0.0)
    t = three - 0.5 * y
    ts = split(t)
    y = dot3(split(y), ts)
    z, zs = t, ts
    ys = split(y)
    t = three - 0.5 * dot3(zs, ys)
    ts = split(t)
    y = dot3(ys, ts)
    z = dot3(ts, zs)
    ys, zs = split(y), split(z)
    t = three - 0.5 * dot3(zs, ys)
    ts = split(t)
    z = dot3(ts, zs)
    return z, y, t, d_col, d_row, inv_row, fro


def gram_of(g_refs, diag_refs):
    total = (g_refs[0][...] + g_refs[1][...]) + (g_refs[2][...] + g_refs[3][...])
    if diag_refs:
        d0, cross, d1 = diag_refs[0][...], total, diag_refs[1][...]
    else:
        cross, both, on_diag = total[:BW], total[BW : 2 * BW], total[2 * BW : 2 * BW + 1]
        at_row = lax.broadcasted_iota(jnp.int32, (BW, BW), 0)
        at_col = lax.broadcasted_iota(jnp.int32, (BW, BW), 1)
        turned = both.T
        d0 = jnp.where(at_col == at_row, on_diag, jnp.where(at_col > at_row, both, turned))
        d1 = jnp.where(at_col > at_row, turned, both)
    top = jnp.concatenate([d0, cross], axis=1)
    bottom = jnp.concatenate([cross.T, d1], axis=1)
    return jnp.concatenate([top, bottom], axis=0)


HALVES = "halves"
CROSSED = (False, True)
SHADOW = (True, False)
PLAIN = (False, False)


PIECES = (RB,)


def rows_of(x_ref, at):
    if isinstance(x_ref, list):
        for piece in x_ref:
            if at < piece.shape[1]:
                return piece[:, at : at + CH]
            at -= piece.shape[1]
    return x_ref[:, at : at + CH]


def columns(x_refs, form, half, j):
    if form == HALVES:
        return x_refs[half][:, j : j + CH]
    ats = [((1 - half) if crossed else half) * RH + j for crossed in form]
    return jnp.concatenate([rows_of(x_ref, at) for x_ref, at in zip(x_refs, ats)], axis=0)


def apply_to(w, x_refs, form, out_ref, offset=None):
    wh, wl = split(w)
    both = jnp.concatenate([wh, wl], axis=0)
    for half in range(2):
        for j in range(0, RH, CH):
            xh, xl = split(columns(x_refs, form, half, j))
            wide = mxu(both, xh)
            value = wide[:BW] + (wide[BW:] + mxu(wh, xl))
            if offset is None:
                out_ref[:, half * RH + j : half * RH + j + CH] = value
            else:
                at = pl.multiple_of((offset if half == 0 else RH - offset) + j, 128)
                out_ref[:, pl.ds(at, CH)] = value


BLOCK = jax.ShapeDtypeStruct((BW, RB), F32)
ROWS_OF_W = jax.ShapeDtypeStruct((BW, PW), F32)
SQUARE = jax.ShapeDtypeStruct((PW, PW), F32)
SCALES = jax.ShapeDtypeStruct((PW, BW), F32)
DIAGONAL = jax.ShapeDtypeStruct((BW, BW), F32)


def call(kernel, ins, outs, name, args):
    return pl.pallas_call(
        kernel,
        in_specs=ins,
        out_specs=[VMEM] * len(outs),
        out_shape=outs,
        compiler_params=params(),
        cost_estimate=cost(10**9, 6 * 10**6),
        name=name,
    )(*args)


def whiten_kernel(first_round, *refs):
    n = 4 if first_round else 6
    g_refs, diag_refs = refs[:4], refs[4:n]
    first_ref, second_ref, z_ref, y_ref, t_ref, d_ref = refs[-6:]
    z, y, t, d_col, d_row, inv_row, fro = newton(gram_of(g_refs, diag_refs))
    wt = jnp.sqrt(d_col) * z.T * (inv_row / jnp.sqrt(fro))
    if first_round:
        apply_to(wt[BW:], refs[n : n + 2], HALVES, second_ref)
        apply_to(wt[:BW], refs[n : n + 2], HALVES, first_ref)
    else:
        first_ref[...] = wt[:BW]
        second_ref[...] = wt[BW:]
    z_ref[...] = z
    y_ref[...] = y
    t_ref[...] = t
    root = jnp.sqrt(d_col) * jnp.sqrt(d_row)
    d_ref[...] = jnp.concatenate([root[:BW, :BW], root[BW:, BW:]], axis=0)


def whiten(grams, diags, xs=(), arrived=()):
    args = [*grams, *diags, *xs, *arrived]
    ins = [VMEM] * (len(args) - len(arrived)) + [ANY] * len(arrived)
    outs = [BLOCK if xs else ROWS_OF_W] * 2 + [SQUARE, SQUARE, SQUARE, SCALES]
    return call(functools.partial(whiten_kernel, bool(xs)), ins, outs, "whiten", args)


def next_diagonals(z_ref, y_ref, t_ref, d_ref):
    ys = split(dot3(split(y_ref[...]), split(t_ref[...])))
    new = dot3(ys, split(z_ref[...]))
    return new[:BW, :BW] * d_ref[:BW], new[BW:, BW:] * d_ref[BW:]


def diagonals_kernel(z_ref, y_ref, t_ref, d_ref, diag0_ref, diag1_ref):
    diag0_ref[...], diag1_ref[...] = next_diagonals(z_ref, y_ref, t_ref, d_ref)


def diagonals(*args):
    return call(diagonals_kernel, [VMEM] * 4, [DIAGONAL, DIAGONAL], "diagonals", args)


def kept_second_kernel(form, w_ref, z_ref, y_ref, t_ref, d_ref, x0_ref, x1_ref, kept_ref, diag_ref, more_ref):
    apply_to(w_ref[...], (x0_ref, x1_ref), form, kept_ref)
    more_ref[:, :BW], diag_ref[...] = next_diagonals(z_ref, y_ref, t_ref, d_ref)
    more_ref[:, BW:] = w_ref[...]


def kept_second(form, *args):
    more = jax.ShapeDtypeStruct((BW, BW + PW), F32)
    kernel = functools.partial(kept_second_kernel, form)
    return call(kernel, [VMEM] * 7, [BLOCK, DIAGONAL, more], "kept_second", args)


def on_second_core_kernel(form, core_ref, w_ref, x0_ref, x1_ref, out_ref, *piece_refs):
    @pl.when(core_ref[0] != 0)
    def _():
        apply_to(w_ref[...], (x0_ref, x1_ref), form, out_ref)
        at = 0
        for piece_ref in piece_refs:
            piece_ref[...] = out_ref[:, at : at + piece_ref.shape[1]]
            at += piece_ref.shape[1]


def on_second_core(form, core, w, xs, name, pieces=()):
    kernel = functools.partial(on_second_core_kernel, form)
    outs = [BLOCK] + [jax.ShapeDtypeStruct((BW, piece), F32) for piece in pieces]
    return call(kernel, [SMEM] + [VMEM] * 3, outs, name, [core, w, *xs])


def combine_kernel(form, n, core_ref, w_ref, *refs):
    s0_ref = list(refs[:n])
    s1_ref, other_ref, kept_ref = refs[n : n + 3]
    in_ref, out_ref = refs[-2:]

    @pl.when(core_ref[0] == 0)
    def _():
        in_ref[:, :RH] = other_ref[:, RH:]
        in_ref[:, RH:] = other_ref[:, :RH]

    @pl.when(core_ref[0] != 0)
    def _():
        apply_to(w_ref[...], (s0_ref, s1_ref), form, in_ref)

    total = jnp.zeros((PW, PW), F32)
    for j in range(0, RB, CH):
        a = jnp.concatenate(split(in_ref[:, j : j + CH]), axis=0)
        b = jnp.concatenate(split(kept_ref[:, j : j + CH]), axis=0)
        total += mxu(a, b, NT)
    out_ref[...] = (total[:BW, :BW] + total[BW:, BW:]) + (total[:BW, BW:] + total[BW:, :BW])


def combine(form, core, w, shadow, other, kept, *arrived):
    pieces, second = shadow
    kernel = functools.partial(combine_kernel, form, len(pieces))
    args = [core, w, *pieces, second, other, kept, *arrived]
    ins = [SMEM] + [VMEM] * (len(pieces) + 4) + [ANY] * len(arrived)
    return call(kernel, ins, [BLOCK, DIAGONAL], "combine", args)


def by_core(w, even):
    parts = [w[i : i + 32] for i in range(0, PW, 32)]
    evens = jnp.concatenate(parts[0::2], axis=0)
    odds = jnp.concatenate(parts[1::2], axis=0)
    return jnp.where(even, evens, odds)


def last_kernel(core_ref, thr_ref, *refs):
    g_refs, diag_refs, x_refs = refs[:4], refs[4:6], refs[6:8]
    send_ref, w_ref = refs[8:]
    core = core_ref[0]
    z, y, t, d_col, d_row, inv_row, fro = newton(gram_of(g_refs, diag_refs))
    y = dot3(split(y), split(t))
    norm = jnp.sqrt(d_col * jnp.sum(z * y, axis=1, keepdims=True) + 1e-06)
    at_row = lax.broadcasted_iota(jnp.int32, (PW, PW), 0)
    at_col = lax.broadcasted_iota(jnp.int32, (PW, PW), 1)
    thr_row = jnp.where(core == 0, thr_ref[:, :PW], thr_ref[:, PW:])
    thr = jnp.sum(jnp.where(at_row == at_col, thr_row, 0.0), axis=1, keepdims=True)
    factor = jnp.maximum(norm - thr, 0.0) / norm
    wt = (factor * jnp.sqrt(d_col)) * z.T * (inv_row / jnp.sqrt(fro))
    apply_to(by_core(wt, core != 0), x_refs, PLAIN, send_ref, core * RH)
    w_ref[...] = by_core(wt, core == 0)


def last(core, thr, grams, diags, xs):
    return pl.pallas_call(
        last_kernel,
        in_specs=[SMEM] + [VMEM] * 9,
        out_specs=[VMEM] * 2,
        out_shape=[jax.ShapeDtypeStruct((BW, RB), F32), jax.ShapeDtypeStruct((BW, PW), F32)],
        compiler_params=params(),
        cost_estimate=cost(10**9, 6 * 10**6),
        name="last",
    )(core, thr, *grams, *diags, *xs)


def last_kept_kernel(core_ref, w_ref, k_ref, m_ref, got_ref, out_ref):
    core = core_ref[0]
    wh, wl = split(w_ref[...])
    both = jnp.concatenate([wh, wl], axis=0)
    mine, other = core * 4, 4 - core * 4
    for half in range(2):
        for j in range(0, RH, CH):
            xh, xl = split(columns((k_ref, m_ref), PLAIN, half, j))
            wide = mxu(both, xh)
            value = wide[:BW] + (wide[BW:] + mxu(wh, xl))
            at = pl.multiple_of((core * RH if half == 0 else RH - core * RH) + j, 128)
            for d in range(32):
                out_ref[d % 8 * 8 + d // 8 + mine, :, pl.ds(at, CH)] = value[4 * d : 4 * d + 4]
    for j in range(0, RB, CH):
        for d in range(32):
            out_ref[d % 8 * 8 + d // 8 + other, :, j : j + CH] = got_ref[4 * d : 4 * d + 4, j : j + CH]


def last_kept(core, w, xs, got):
    return pl.pallas_call(
        last_kept_kernel,
        in_specs=[SMEM] + [VMEM] * 4,
        out_specs=VMEM,
        out_shape=jax.ShapeDtypeStruct((64, 4, RB), F32),
        compiler_params=params(),
        cost_estimate=cost(10**9, 6 * 10**6),
        name="last_kept",
    )(core, w, *xs, got)


def place_kernel(in_ref, out_ref):
    for w in range(4):
        for j in range(0, RB, CH):
            rows = in_ref[:, 0, w, j : j + CH]
            out_ref[8 * w : 8 * w + 8, j : j + CH] = jnp.concatenate([rows[7:], rows[:7]], axis=0)


def place(landed):
    return pl.pallas_call(
        place_kernel,
        grid=(8,),
        in_specs=[pl.BlockSpec((8, 1, 4, RB), lambda i: (0, i, 0, 0))],
        out_specs=pl.BlockSpec((32, RB), lambda i: (0, i)),
        out_shape=jax.ShapeDtypeStruct((32, 8 * RB), F32),
        compiler_params=params(),
        cost_estimate=cost(10**6, 6 * 10**6),
        name="place",
    )(landed)


def to(block, where):
    route = []
    for i in range(8):
        for c in range(2):
            for g in range(8):
                goal = where(i, c, g)
                if goal is not None:
                    ti, tc, tg = goal
                    route.append(((i * 2 + c) * 8 + g, (ti * 2 + tc) * 8 + tg))
    return lax.ppermute(block, AXES, route)


def swap_cores(block):
    return to(block, lambda i, c, g: (i, 1 - c, g))


def onward(block):
    return to(block, lambda i, c, g: (i, 1, g) if c == 0 else (i, 0, (g + 1) % 8))


def backward(block):
    return to(block, lambda i, c, g: (i, 1, (g - 1) % 8) if c == 0 else (i, 0, g))


def behind(block, core):
    return to(block, lambda i, c, g: (i, 1, (g - 1) % 8) if c == core else None)


def beside(block):
    return to(block, lambda i, c, g: (i, 0, g) if c == 1 else None)


def reduced(partial):
    pair = partial + to(partial, lambda i, c, g: (i ^ 1, c, g))
    return [pair] + [to(pair, lambda i, c, g, k=k: (i ^ k, c, g)) for k in (2, 4, 6)]


def on_device(observed, estimate, mask, threshold):
    core = lax.axis_index("core").reshape(1).astype(jnp.int32)
    thr = to(threshold.reshape(1, -1), lambda i, c, g: (i, c, (g - 1) % 8))
    keep, send = fill(core, observed, estimate, mask)
    got = swap_cores(send)
    grams = reduced(gram_second(got, *gram_first(keep)))
    first, second, *rest = whiten(grams, [], (keep, got))
    joined = onward(second)
    back = behind(first, 0)
    diag0, diag1 = diagonals(*rest)
    diags = [diag0, onward(diag1)]
    partial = gram_cross(first, joined, back, thr)
    xs = (first, joined)
    w0, w1, *rest = whiten(reduced(partial), diags)
    w_shadow = behind(w0, 0)
    (given,) = on_second_core(CROSSED, core, w0, xs, "given")
    other = beside(given)
    pieces = [behind(given, 1)]
    kept, diag1, more = kept_second(CROSSED, w1, *rest, *xs)
    more = backward(more)
    joined, partial = combine(SHADOW, core, w_shadow, ([back], second), other, kept)
    (moved,) = on_second_core(SHADOW, core, more[:, BW:], (back, second), "shadow")
    diags = [more[:, :BW], diag1]
    xs = (joined, kept)
    w0, w1, *rest = whiten(reduced(partial), diags)
    w_shadow = behind(w0, 0)
    (given,) = on_second_core(PLAIN, core, w0, xs, "given")
    other = beside(given)
    kept, diag1, more = kept_second(PLAIN, w1, *rest, *xs)
    more = backward(more)
    joined, partial = combine(PLAIN, core, w_shadow, (pieces, moved), other, kept)
    diags = [more[:, :BW], diag1]
    xs = (joined, kept)
    send, w = last(core, thr, reduced(partial), diags, xs)
    got = swap_cores(send)
    packed = last_kept(core, w, xs, got)
    landed = lax.all_to_all(packed, ("pairs", "zx"), split_axis=0, concat_axis=0, tiled=True)
    return place(landed.reshape(8, 8, 4, RB))


def solution(mesh):
    finer = Mesh(mesh.devices.reshape(8, 2, 8), AXES)
    placed = P(("zx", "core"), "pairs")
    return jax.shard_map(
        on_device,
        mesh=finer,
        in_specs=(placed, placed, placed, P("pairs")),
        out_specs=P(AXES, None),
        check_vma=False,
    )
```
